256 devices in a mesh: fsdp: 32 (over y, z), tp: 8 (over x, core).
Axes of the slice: x: 4, y: 4, z: 8, core: 2. Of those that a mesh axis runs over, the one named last changes fastest.
Arguments:
- momentum: float32 [8192, 26624], P('fsdp', 'tp'), may hold values from -122 to 122, as said below
- gradient: bfloat16 [8192, 26624], P('fsdp', 'tp'), may hold values from -6 to 6
- basis: float32 [256, 26624], P('fsdp', 'tp'), may hold values from -0.0390625 to 0.0390625
Outputs:
- new_momentum: float32 [8192, 26624], P('fsdp', 'tp')
- new_basis: float32 [256, 26624], P('fsdp', 'tp')
- step: bfloat16 [8192, 26624], P('fsdp', 'tp')
The draws below stay inside these ranges and needn't reach their ends.
Inputs may be any that keep to these rules, and one draw needn't show every extreme that they name: `momentum`: momentum entries are finite real values.
All inputs are finite; a program needn't handle non-finite values.
Results may differ from the reference program's by a relative error of at most 0.004.
Values sent between devices are 32-bit elements; how exact they have to be, the bound alone decides.
A program may use at most 64 MiB of HBM per device.

```python
import jax
import jax.numpy as jnp
from jax import lax

ROWS = 8192
COLS = 26624
RANK = 256


def ramp_scale(key, length, low, high):
    level = jax.random.uniform(key, (length,), jnp.float32, jnp.log(low), jnp.log(high))
    slope = 1.0 + 2.0 * jnp.arange(length, dtype=jnp.float32) / length
    return jnp.exp(level) * slope


def draw_momentum(key, part):
    key = jax.random.fold_in(key, 7)
    base_key, row_key, col_key = jax.random.split(key, 3)
    base = jnp.clip(jax.random.normal(base_key, (ROWS, COLS), jnp.float32), -6.0, 6.0)
    row_scale = ramp_scale(row_key, ROWS, 0.3, 3.0)
    col_scale = ramp_scale(col_key, COLS, 0.3, 3.0)
    return 0.25 * base * row_scale[:, None] * col_scale[None, :]


def steps_of(own_key, extent, pieces, low, high):
    gain, own = 1.0, jax.random.fold_in(own_key, 6)
    for position, parts in pieces:
        steps = jnp.exp(jax.random.uniform(jax.random.fold_in(own, position), (parts,), jnp.float32, low / len(pieces), high / len(pieces)))
        gain = gain * jnp.repeat(steps, extent[position] // parts).reshape([-1 if axis == position else 1 for axis in range(len(extent))])
    return gain


def gaussian(own_key, dims, scale, reach, cuts=(), kind=jnp.bfloat16):
    factor_of = steps_of(own_key, dims, cuts, -0.22, 0.18) if cuts else 1.0
    entries = jax.random.normal(own_key, dims, jnp.float32) * scale * factor_of
    return jnp.minimum(jnp.maximum(entries, -reach), reach).astype(kind)


def setup_inputs(seed: int = 0) -> dict:
    seeds = jax.random.split(jax.random.key(seed), 4)
    momentum = draw_momentum(jax.random.fold_in(seeds[3], 71), 0)
    gradient = gaussian(seeds[1], (ROWS, COLS), 1.0, 6.0, ((0, 32), (1, 8)))
    basis = gaussian(seeds[2], (RANK, COLS), COLS ** -0.5, 0.0390625, ((0, 32), (1, 8)), jnp.float32)
    return dict(momentum=momentum, gradient=gradient, basis=basis)


momentum_decay = 0.95
norm_eps = 1e-06

def mat(left, right):
    return jnp.dot(left.astype(jnp.float32), right.astype(jnp.float32), precision=lax.Precision.HIGHEST, preferred_element_type=jnp.float32)

def reference(momentum, gradient, basis):
    buffer = momentum + gradient.astype(jnp.float32)
    projected = mat(buffer, basis.T)
    gram_matrix = mat(projected.T, projected)
    factor = jnp.linalg.cholesky(gram_matrix)
    ortho_basis = lax.linalg.triangular_solve(factor, projected, left_side=False, lower=True, transpose_a=True)
    coeffs = mat(ortho_basis.T, buffer)
    inverse_norm = lax.rsqrt(lax.optimization_barrier(jnp.sum(coeffs * coeffs, axis=1)) + norm_eps)
    new_basis = coeffs * inverse_norm[:, None]
    new_momentum = buffer - (1.0 - momentum_decay) * mat(ortho_basis, coeffs)
    scale = (ROWS * COLS / RANK) ** 0.5
    step = (scale * mat(ortho_basis * inverse_norm[None, :], coeffs)).astype(jnp.bfloat16)
    return (new_momentum, new_basis, step)
```

```python
import functools

import jax
import jax.numpy as jnp
from jax import lax
from jax.experimental import pallas as pl
from jax.experimental.pallas import tpu as pltpu
from jax.sharding import PartitionSpec as P

ROWS = 8192
COLS = 26624
RANK = 256

momentum_decay = 0.95
norm_eps = 1e-06

Y, Z, T = 4, 8, 8
F = Y * Z
M = ROWS // F
N = COLS // T
R = RANK // F
BLOCK = 256
NB = 16

CUT = 1536
A = (0, CUT)
A_HALF = ((0, CUT // 2), (CUT // 2, CUT // 2))
B = (CUT, N - CUT)
B_HALF = ((CUT, (N - CUT) // 2), (CUT + (N - CUT) // 2, (N - CUT) // 2))

MESH = pl.DeviceIdType.MESH
f32, bf16 = jnp.float32, jnp.bfloat16


def split(value):
    high = value.astype(bf16)
    return high, (value - high.astype(f32)).astype(bf16)


def dot(left, right, dims=((1,), (0,))):
    return lax.dot_general(left, right, (dims, ((), ())), preferred_element_type=f32)


def dot3(left, right, dims=((1,), (0,))):
    (lh, ll), (rh, rl) = left, right
    return dot(lh, rh, dims) + (dot(lh, rl, dims) + dot(ll, rh, dims))


def exact(left, right, dims=((1,), (0,))):
    return lax.dot_general(
        left, right, (dims, ((), ())), precision=lax.Precision.HIGHEST, preferred_element_type=f32
    )


class Wires:
    def __init__(self, send, recv):
        self.send, self.recv, self.count, self.sent = send, recv, 0, []

    def start(self, src, dst, to):
        copy = pltpu.make_async_remote_copy(
            src_ref=src,
            dst_ref=dst,
            send_sem=self.send.at[self.count],
            recv_sem=self.recv.at[self.count],
            device_id=to,
            device_id_type=MESH,
        )
        self.count += 1
        copy.start()
        self.sent.append(copy)
        return copy

    def drain(self, copies=None):
        for copy in list(self.sent if copies is None else copies):
            copy.wait_send()
            self.sent = [other for other in self.sent if other is not copy]


class Place:
    def __init__(self):
        self.f = lax.axis_index("fsdp")
        self.t = lax.axis_index("tp")
        self.y, self.z = self.f // Z, self.f % Z

    def slot(self, dy, dz):
        return (self.y + dy + Y) % Y * Z + (self.z + dz + Z) % Z

    def along_y(self, d):
        return {"fsdp": self.slot(d, 0)}

    def along_z(self, d):
        return {"fsdp": self.slot(0, d)}

    def along_t(self, d):
        return {"tp": (self.t + d) % T}


def cols(ref, slot, part):
    return ref.at[slot, :, pl.ds(part[0], part[1])]


def gather_steps(place, wires, buf):
    a1, b1, a2, b2 = {}, {}, {}, {}
    a_order = (0, -1, 1, 2)
    b_order = (0, -1, 1, -2, 2, -3, 3, 4)
    at = place.slot

    def send(book, key, slot, part, to):
        book[key] = wires.start(cols(buf, slot, part), cols(buf, slot, part), to)

    def a2_step(i):
        h, k = i // 4 + 1, i % 4
        for side, d in enumerate((1, -1)):
            if h > 1:
                a2[h - 1, k, d].wait_recv()
            part = A_HALF[side] if h == 4 else A
            send(a2, (h, k, d), at(a_order[k], -d * (h - 1)), part, place.along_z(d))

    def b2_step(i):
        h, k = i // 8 + 1, i % 8
        for side, d in enumerate((1, -1)):
            if h == 2:
                b2[1, k, d].wait_recv()
            part = B_HALF[side] if h == 2 else B
            send(b2, (h, k, d), at(-d * (h - 1), b_order[k]), part, place.along_y(d))

    def a1_step(i):
        if i == 0:
            for d in (1, -1):
                send(a1, (1, d), at(0, 0), A, place.along_y(d))
        elif i in (1, 2):
            side, d = i - 1, (1, -1)[i - 1]
            a1[1, d].wait_recv()
            send(a1, (2, d), at(-d, 0), A_HALF[side], place.along_y(d))
        elif i == 3:
            for d in (1, -1):
                a1[2, d].wait_recv()

    def b1_step(i):
        if i == 0:
            for d in (1, -1):
                send(b1, (1, d), at(0, 0), B, place.along_z(d))
        elif i in range(1, 7):
            h, side = (i + 1) // 2, (i + 1) % 2
            d = (1, -1)[side]
            b1[h, d].wait_recv()
            part = B_HALF[side] if h == 3 else B
            send(b1, (h + 1, d), at(0, -d * h), part, place.along_z(d))
        elif i == 7:
            for d in (1, -1):
                b1[4, d].wait_recv()

    def step(i):
        b1_step(i)
        a1_step(i)
        b2_step(i)
        a2_step(i)

    def last():
        for k in range(4):
            for d in (1, -1):
                a2[4, k, d].wait_recv()
        for k in range(8):
            for d in (1, -1):
                b2[2, k, d].wait_recv()

    return [functools.partial(step, i) for i in range(16)] + [last]


def scatter_steps(place, wires, part_sums, result, land_a, land_b):
    a1, b1, a2, b2 = {}, {}, {}, {}
    a_order = (2, 1, -1, 0)
    b_order = (4, 3, -3, 2, -2, 1, -1, 0)
    at = place.slot
    used = {"a": 0, "b": 0}

    def send(book, key, slot, part, to, kind):
        land = land_a if kind == "a" else land_b
        index, offset = used[kind], part[0] - (A if kind == "a" else B)[0]
        used[kind] += 1
        target = land.at[index, :, pl.ds(offset, part[1])]
        book[key] = (wires.start(cols(part_sums, slot, part), target, to), target, part)

    def add(book, key, slot):
        copy, target, part = book[key]
        copy.wait_recv()
        own = cols(part_sums, slot, part)
        own[...] += target[...]

    def a1_step(i):
        h, k = i // 4 + 1, i % 4
        for side, d in enumerate((1, -1)):
            slot = at(a_order[k], d * (5 - h))
            if h > 1:
                add(a1, (h - 1, k, d), slot)
            part = A_HALF[side] if h == 1 else A
            send(a1, (h, k, d), slot, part, place.along_z(d), "a")

    def b1_step(i):
        h, k = i // 8 + 1, i % 8
        for side, d in enumerate((1, -1)):
            slot = at(d * (3 - h), b_order[k])
            if h == 2:
                add(b1, (1, k, d), slot)
            part = B_HALF[side] if h == 1 else B
            send(b1, (h, k, d), slot, part, place.along_y(d), "b")

    def a1_end(k):
        for d in (1, -1):
            add(a1, (4, k, d), at(a_order[k], 0))

    def b1_end(k):
        for d in (1, -1):
            add(b1, (2, k, d), at(0, b_order[k]))

    def a2_step(h):
        for side, d in enumerate((1, -1)):
            slot = at(d * (3 - h), 0)
            if h == 2:
                add(a2, (1, d), slot)
            send(a2, (h, d), slot, A_HALF[side] if h == 1 else A, place.along_y(d), "a")

    def b2_step(h):
        for side, d in enumerate((1, -1)):
            slot = at(0, d * (5 - h))
            if h > 1:
                add(b2, (h - 1, d), slot)
            send(b2, (h, d), slot, B_HALF[side] if h == 1 else B, place.along_z(d), "b")

    def end(book, key, part):
        own = at(0, 0)
        for d in (1, -1):
            add(book, key + (d,), own)
        cols(result, own, part)[...] = cols(part_sums, own, part)[...]

    def step(i):
        if i < 16:
            a1_step(i)
            b1_step(i)
        if 0 <= i - 10 < 8:
            b1_end(i - 10)
        if 0 <= i - 14 < 4:
            a1_end(i - 14)
        if i in (10, 12, 14, 16):
            b2_step((i - 8) // 2)
        if i in (14, 16):
            a2_step((i - 12) // 2)
        if i == 18:
            end(a2, (2,), A)
            end(b2, (4,), B)

    return [functools.partial(step, i) for i in range(19)]


A_LANDS = 4 * 4 * 2 + 2 * 2
B_LANDS = 2 * 8 * 2 + 4 * 2
GATHER_WIRES = 4 + 8 + 32 + 32
SCATTER_WIRES = 32 + 32 + 4 + 8
WIRES = 2 * GATHER_WIRES + SCATTER_WIRES + 7 + 7 + 7 + 3 + 7 + 7 + 7


def column_block(c):
    return pl.ds(pl.multiple_of(c * BLOCK, BLOCK), BLOCK)


def core(
    momentum, gradient, basis,
    coeffs, ortho, inverse, new_basis,
    q_all, w_part, w_all, land_a, land_b, m_buf, g_buf, b_high, b_low,
    p_part, p_land, p_all, p_t, gram_own, gram_z, gram_y, work, linv, norms,
    send, recv, local,
):
    place = Place()
    wires = Wires(send, recv)
    f, t, y, z = place.f, place.t, place.y, place.z

    loads = [
        pltpu.make_async_copy(basis, q_all.at[f], local.at[0]),
        pltpu.make_async_copy(momentum, m_buf, local.at[1]),
        pltpu.make_async_copy(gradient, g_buf, local.at[2]),
    ]
    for load in loads:
        load.start()

    barrier = pltpu.get_barrier_semaphore()
    peers = (
        [place.along_y(d) for d in range(1, Y)]
        + [place.along_z(d) for d in range(1, Z)]
        + [place.along_t(d) for d in range(1, T)]
    )
    for peer in peers:
        pl.semaphore_signal(barrier, inc=1, device_id=peer, device_id_type=MESH)
    pl.semaphore_wait(barrier, len(peers))

    loads[0].wait()
    steps = gather_steps(place, wires, q_all)
    for step in steps[:2]:
        step()
    loads[1].wait()
    loads[2].wait()

    @pl.loop(0, N // BLOCK)
    def _(c):
        at = column_block(c)
        high, low = split(m_buf[:, at] + g_buf[:, at].astype(f32))
        b_high[:, at] = high
        b_low[:, at] = low

    for step in steps[2:]:
        step()

    p_part[...] = jnp.zeros_like(p_part)

    @pl.loop(0, N // BLOCK)
    def _(c):
        at = column_block(c)
        q = split(q_all[:, :, at].reshape(RANK, BLOCK))
        p_part[...] += dot3((b_high[:, at], b_low[:, at]), q, ((1,), (1,))).reshape(T, M // T, RANK)

    copies = []
    for d in range(1, T):
        copies.append(wires.start(p_part.at[(t + d) % T], p_land.at[t], place.along_t(d)))
    p_land[t] = p_part[t]
    for copy in copies:
        copy.wait_recv()
    total = p_land[0]
    for i in range(1, T):
        total = total + p_land[i]
    p_all[t] = total
    copies = [wires.start(p_all.at[t], p_all.at[t], place.along_t(d)) for d in range(1, T)]
    for copy in copies:
        copy.wait_recv()

    proj = p_all[...].reshape(M, RANK)
    p_t[...] = proj.T
    rows = p_t[pl.ds(pl.multiple_of(t * (RANK // T), RANK // T), RANK // T), :]
    own = exact(rows, proj)
    for j in range(Z):
        gram_own[j] = own[8 * (j // 2) : 8 * (j // 2) + 8, 128 * (j % 2) : 128 * (j % 2) + 128]
    gram_copies = [
        wires.start(gram_own.at[(z + d) % Z], gram_z.at[z], place.along_z(d)) for d in range(1, Z)
    ]
    gram_sent = list(gram_copies)
    gram_z[z] = gram_own[z]

    pt_split = split(p_t[...])

    @pl.loop(0, N // BLOCK)
    def _(c):
        at = column_block(c)
        w_part[:, :, at] = dot3(pt_split, (b_high[:, at], b_low[:, at])).reshape(F, R, BLOCK)

    def summed(ref, count):
        total = ref[0]
        for i in range(1, count):
            total = total + ref[i]
        return total

    tile = (4 * t + z // 2, slice(None), pl.ds(pl.multiple_of(z % 2 * 128, 128), 128))

    def gram_1():
        for copy in gram_copies:
            copy.wait_recv()
        gram_y[y] = summed(gram_z, Z)
        gram_copies[:] = [
            wires.start(gram_y.at[y], gram_y.at[y], place.along_y(d)) for d in range(1, Y)
        ]

    def gram_2():
        for copy in gram_copies:
            copy.wait_recv()
        work[tile] = summed(gram_y, Y)
        gram_sent.extend(gram_copies)
        gram_copies[:] = [
            wires.start(work.at[tile], work.at[tile], place.along_z(d)) for d in range(1, Z)
        ]

    def gram_3():
        for copy in gram_copies:
            copy.wait_recv()
        own = work.at[pl.ds(4 * t, 4), :, pl.ds(0, RANK)]
        gram_sent.extend(gram_copies)
        gram_copies[:] = [wires.start(own, own, place.along_t(d)) for d in range(1, T)]

    def gram_4():
        for copy in gram_copies:
            copy.wait_recv()
        wires.drain(gram_sent + gram_copies)
        row = lax.broadcasted_iota(jnp.int32, (RANK, RANK), 0)
        lane = lax.broadcasted_iota(jnp.int32, (RANK, RANK), 1)
        work[:, :, RANK:] = jnp.where(row == lane, 1.0, 0.0).astype(f32).reshape(F, R, RANK)

    lane = lax.broadcasted_iota(jnp.int32, (NB, 128), 1)
    sub = lax.broadcasted_iota(jnp.int32, (NB, 128), 0)

    def panel(p):
        tiles = NB // R
        here = work[pl.ds(p * tiles, tiles)].reshape(NB, 2 * RANK)
        first = p * NB
        low_half = jnp.where(first < 128, here[:, :128], here[:, 128:256])
        block = pltpu.roll(low_half, (128 - first % 128) % 128, 1)
        block = jnp.where(lane < NB, block, jnp.where(lane == sub + NB, 1.0, 0.0))
        diag = jnp.ones((NB, 128), f32)
        for j in range(NB):
            pivot = block[j : j + 1, j : j + 1]
            factor = block[:, j : j + 1] * (1.0 / pivot)
            diag = jnp.where(sub == j, pivot, diag)
            if j < NB - 1:
                block = block - jnp.where(sub > j, factor, 0.0) * block[j : j + 1, :]
        inverse_block = (block * lax.rsqrt(diag))[:, NB : 2 * NB]
        done = exact(inverse_block, here)
        linv[pl.ds(p * tiles, tiles)] = done[:, RANK:].reshape(tiles, R, RANK)
        high = done.astype(bf16).astype(f32)
        mid = (done - high).astype(bf16).astype(f32)
        low = (done - high) - mid
        left = jnp.concatenate([x[:, :RANK] for x in (high, high, mid, high, low, mid)]).astype(bf16)
        right = jnp.concatenate([high, mid, high, low, high, mid]).astype(bf16)
        work[...] -= dot(left, right, ((0,), (0,))).reshape(F, R, 2 * RANK)

    def panels(begin, end):
        def run():
            @pl.loop(begin, end)
            def _(p):
                panel(p)

        return run

    count = RANK // NB
    side = [None, gram_1, None, gram_2, None, gram_3, None, gram_4]
    side += [panels(p, p + 1) for p in range(count)]

    steps = scatter_steps(place, wires, w_part, w_all, land_a, land_b)
    steps = steps + gather_steps(place, wires, w_all)
    for step in steps:
        step()
        if side:
            work_beside = side.pop(0)
            if work_beside is not None:
                work_beside()
    for work_beside in side:
        work_beside()

    factor_inverse = split(linv[...].reshape(RANK, RANK))
    ortho[...] = exact(p_all[...].reshape(M, RANK), linv[...].reshape(RANK, RANK), ((1,), (1,)))
    norms[0] = jnp.zeros((RANK, 128), f32)

    @pl.loop(0, N // BLOCK)
    def _(c):
        at = column_block(c)
        part = dot3(factor_inverse, split(w_all[:, :, at].reshape(RANK, BLOCK)))
        coeffs[:, at] = part
        squares = part * part
        norms[0] += squares[:, :128] + squares[:, 128:]

    norms_t = norms[0].T
    own_norms = jnp.sum(norms_t, axis=0, keepdims=True)
    inverse_land = norms.at[1]
    inverse_land[pl.ds(pl.multiple_of(t * 16, 16), 8), :] = jnp.broadcast_to(own_norms[:, :128], (8, 128))
    inverse_land[pl.ds(pl.multiple_of(t * 16, 16) + 8, 8), :] = jnp.broadcast_to(own_norms[:, 128:], (8, 128))
    mine = inverse_land.at[pl.ds(pl.multiple_of(t * 16, 16), 16), :]
    copies = [wires.start(mine, mine, place.along_t(d)) for d in range(1, T)]
    for copy in copies:
        copy.wait_recv()
    total = inverse_land[0:16, :]
    for i in range(1, T):
        total = total + inverse_land[16 * i : 16 * i + 16, :]
    scale = lax.rsqrt(total + norm_eps)
    inverse_row = jnp.concatenate([scale[0:8], scale[8:16]], axis=1)
    inverse[...] = inverse_row
    lanes = lax.broadcasted_iota(jnp.int32, (R, RANK), 1)
    subs = lax.broadcasted_iota(jnp.int32, (R, RANK), 0)
    own_inverse = jnp.sum(jnp.where(lanes == subs + f * R, inverse_row, 0.0), axis=1, keepdims=True)
    new_basis[...] = coeffs[pl.ds(pl.multiple_of(f * R, R), R), :] * own_inverse
    wires.drain()
    assert wires.count == WIRES


def core_call(momentum, gradient, basis):
    any_space = pl.BlockSpec(memory_space=pl.ANY)
    vmem = pl.BlockSpec(memory_space=pltpu.VMEM)
    return pl.pallas_call(
        core,
        out_shape=(
            jax.ShapeDtypeStruct((RANK, N), f32),
            jax.ShapeDtypeStruct((M, RANK), f32),
            jax.ShapeDtypeStruct((8, RANK), f32),
            jax.ShapeDtypeStruct((R, N), f32),
        ),
        in_specs=[any_space] * 3,
        out_specs=(vmem,) * 4,
        scratch_shapes=[
            pltpu.VMEM((F, R, N), f32),
            pltpu.VMEM((F, R, N), f32),
            pltpu.VMEM((F, R, N), f32),
            pltpu.VMEM((A_LANDS, R, A[1]), f32),
            pltpu.VMEM((B_LANDS, R, B[1]), f32),
            pltpu.VMEM((M, N), f32),
            pltpu.VMEM((M, N), bf16),
            pltpu.VMEM((M, N), bf16),
            pltpu.VMEM((M, N), bf16),
            pltpu.VMEM((T, M // T, RANK), f32),
            pltpu.VMEM((T, M // T, RANK), f32),
            pltpu.VMEM((T, M // T, RANK), f32),
            pltpu.VMEM((RANK, M), f32),
            pltpu.VMEM((Z, 8, 128), f32),
            pltpu.VMEM((Z, 8, 128), f32),
            pltpu.VMEM((Y, 8, 128), f32),
            pltpu.VMEM((F, R, 2 * RANK), f32),
            pltpu.VMEM((F, R, RANK), f32),
            pltpu.VMEM((2, RANK, 128), f32),
            pltpu.SemaphoreType.DMA((WIRES,)),
            pltpu.SemaphoreType.DMA((WIRES,)),
            pltpu.SemaphoreType.DMA((3,)),
        ],
        compiler_params=pltpu.CompilerParams(
            collective_id=0, has_side_effects=True, vmem_limit_bytes=56 * 2**20
        ),
        name="core",
    )(momentum, gradient, basis)


def update(momentum, gradient, coeffs, ortho, inverse, new_momentum, step):
    buffer = momentum[...] + gradient[...].astype(f32)
    high, low = split(coeffs[...])
    basis = ortho[...]
    new_momentum[...] = buffer - (1.0 - momentum_decay) * dot(basis.astype(bf16), high)
    scale = (ROWS * COLS / RANK) ** 0.5
    scaled = split(basis * (inverse[0:1, :] * scale))
    step[...] = dot3(scaled, (high, low)).astype(bf16)


def update_call(momentum, gradient, coeffs, ortho, inverse):
    def block(rows):
        return pl.BlockSpec((rows, BLOCK), lambda c: (0, c))

    return pl.pallas_call(
        update,
        grid=(N // BLOCK,),
        out_shape=(jax.ShapeDtypeStruct((M, N), f32), jax.ShapeDtypeStruct((M, N), bf16)),
        in_specs=[
            block(M), block(M), block(RANK),
            pl.BlockSpec((M, RANK), lambda c: (0, 0)),
            pl.BlockSpec((8, RANK), lambda c: (0, 0)),
        ],
        out_specs=(block(M), block(M)),
        name="update",
    )(momentum, gradient, coeffs, ortho, inverse)


def on_device(momentum, gradient, basis):
    coeffs, ortho, inverse, new_basis = core_call(momentum, gradient, basis)
    new_momentum, step = update_call(momentum, gradient, coeffs, ortho, inverse)
    return (new_momentum, new_basis, step)


def solution(mesh):
    placed = (P("fsdp", "tp"), P("fsdp", "tp"), P("fsdp", "tp"))
    return jax.shard_map(
        on_device,
        mesh=mesh,
        in_specs=placed,
        out_specs=(P("fsdp", "tp"), P("fsdp", "tp"), P("fsdp", "tp")),
        check_vma=False,
    )
```

```python
import functools

import jax
import jax.numpy as jnp
from jax import lax
from jax.experimental import pallas as pl
from jax.experimental.pallas import tpu as pltpu
from jax.sharding import PartitionSpec as P

ROWS = 8192
COLS = 26624
RANK = 256

momentum_decay = 0.95
norm_eps = 1e-06

Y, Z, T = 4, 8, 8
F = Y * Z
M = ROWS // F
N = COLS // T
R = RANK // F
BLOCK = 256
NB = 16


class Part:
    def __init__(self, begin, size, cut):
        self.begin, self.size = begin, size
        self.a, self.b = (begin, cut), (begin + cut, size - cut)
        self.a_half, self.b_half = self.halves(self.a), self.halves(self.b)

    @staticmethod
    def halves(part):
        first = (part[1] // 128 + 1) // 2 * 128
        return (part[0], first), (part[0] + first, part[1] - first)


PART = Part(0, N, 1408)
A_LANDS = 4 * 4 * 2 + 2 * 2
B_LANDS = 2 * 8 * 2 + 4 * 2
POOL = 40
SHIFT = 2

MESH = pl.DeviceIdType.MESH
f32, bf16 = jnp.float32, jnp.bfloat16


def split(value):
    high = value.astype(bf16)
    return high, (value - high.astype(f32)).astype(bf16)


def dot(left, right, dims=((1,), (0,))):
    return lax.dot_general(left, right, (dims, ((), ())), preferred_element_type=f32)


def dot3(left, right, dims=((1,), (0,))):
    (lh, ll), (rh, rl) = left, right
    return dot(lh, rh, dims) + (dot(lh, rl, dims) + dot(ll, rh, dims))


def exact(left, right, dims=((1,), (0,))):
    return lax.dot_general(
        left, right, (dims, ((), ())), precision=lax.Precision.HIGHEST, preferred_element_type=f32
    )


class Wires:
    def __init__(self, send, recv):
        self.send, self.recv = send, recv
        self.sent, self.used = {}, 0

    def range(self, begin, count):
        indices = iter(range(begin, begin + count))
        return lambda src, dst, to: self.start(src, dst, to, next(indices))

    def start(self, src, dst, to, index):
        place = self.used % POOL
        self.wait_sent(self.sent.get(place))
        copy = pltpu.make_async_remote_copy(
            src_ref=src,
            dst_ref=dst,
            send_sem=self.send.at[place],
            recv_sem=self.recv.at[index],
            device_id=to,
            device_id_type=MESH,
        )
        copy.start()
        self.sent[place] = copy
        self.used += 1
        return copy

    def wait_sent(self, copy):
        for place, other in list(self.sent.items()):
            if other is copy:
                copy.wait_send()
                del self.sent[place]

    def drain(self, copies=None):
        for copy in list(self.sent.values()) if copies is None else copies:
            self.wait_sent(copy)


class Place:
    def __init__(self):
        self.f = lax.axis_index("fsdp")
        self.t = lax.axis_index("tp")
        self.y, self.z = self.f // Z, self.f % Z
        self.x, self.c = self.t // 2, self.t % 2

    def slot(self, dy, dz):
        return (self.y + dy + Y) % Y * Z + (self.z + dz + Z) % Z

    def along_y(self, d):
        return {"fsdp": self.slot(d, 0)}

    def along_z(self, d):
        return {"fsdp": self.slot(0, d)}

    def along_x(self, d):
        return {"tp": (self.x + d) % 4 * 2 + self.c}

    def other_core(self):
        return {"tp": self.x * 2 + 1 - self.c}


def cols(ref, slot, part):
    return ref.at[slot, :, pl.ds(part[0], part[1])]


def gather_steps(place, start, buf, part):
    a1, b1, a2, b2 = {}, {}, {}, {}
    a_order = (0, -1, 1, 2)
    b_order = (0, -1, 1, -2, 2, -3, 3, 4)
    at = place.slot

    def send(book, key, slot, piece, to):
        book[key] = start(cols(buf, slot, piece), cols(buf, slot, piece), to)

    def a2_step(i):
        h, k = i // 4 + 1, i % 4
        for side, d in enumerate((1, -1)):
            if h > 1:
                a2[h - 1, k, d].wait_recv()
            piece = part.a_half[side] if h == 4 else part.a
            send(a2, (h, k, d), at(a_order[k], -d * (h - 1)), piece, place.along_z(d))

    def b2_step(i):
        h, k = i // 8 + 1, i % 8
        for side, d in enumerate((1, -1)):
            if h == 2:
                b2[1, k, d].wait_recv()
            piece = part.b_half[side] if h == 2 else part.b
            send(b2, (h, k, d), at(-d * (h - 1), b_order[k]), piece, place.along_y(d))

    def a1_step(i):
        if i == 0:
            for d in (1, -1):
                send(a1, (1, d), at(0, 0), part.a, place.along_y(d))
        elif i in (1, 2):
            side, d = i - 1, (1, -1)[i - 1]
            a1[1, d].wait_recv()
            send(a1, (2, d), at(-d, 0), part.a_half[side], place.along_y(d))
        elif i == 3:
            for d in (1, -1):
                a1[2, d].wait_recv()

    def b1_step(i):
        if i == 0:
            for d in (1, -1):
                send(b1, (1, d), at(0, 0), part.b, place.along_z(d))
        elif i in range(1, 7):
            h, side = (i + 1) // 2, (i + 1) % 2
            d = (1, -1)[side]
            b1[h, d].wait_recv()
            piece = part.b_half[side] if h == 3 else part.b
            send(b1, (h + 1, d), at(0, -d * h), piece, place.along_z(d))
        elif i == 7:
            for d in (1, -1):
                b1[4, d].wait_recv()

    def step(i):
        b1_step(i)
        a1_step(i)
        b2_step(i)
        a2_step(i)

    def last():
        for k in range(4):
            for d in (1, -1):
                a2[4, k, d].wait_recv()
        for k in range(8):
            for d in (1, -1):
                b2[2, k, d].wait_recv()

    return [functools.partial(step, i) for i in range(16)] + [last]


def scatter_steps(place, start, part_sums, result, land_a, land_b, part):
    a1, b1, a2, b2 = {}, {}, {}, {}
    a_order = (2, 1, -1, 0)
    b_order = (4, 3, -3, 2, -2, 1, -1, 0)
    at = place.slot
    used = {"a": 0, "b": 0}

    def send(book, key, slot, piece, to, kind):
        land = land_a if kind == "a" else land_b
        index, offset = used[kind], piece[0] - (part.a if kind == "a" else part.b)[0]
        used[kind] += 1
        target = land.at[index, :, pl.ds(offset, piece[1])]
        book[key] = (start(cols(part_sums, slot, piece), target, to), target, piece)

    def add(book, key, slot):
        copy, target, piece = book[key]
        copy.wait_recv()
        own = cols(part_sums, slot, piece)
        own[...] += target[...]

    def a1_step(i):
        h, k = i // 4 + 1, i % 4
        for side, d in enumerate((1, -1)):
            slot = at(a_order[k], d * (5 - h))
            if h > 1:
                add(a1, (h - 1, k, d), slot)
            piece = part.a_half[side] if h == 1 else part.a
            send(a1, (h, k, d), slot, piece, place.along_z(d), "a")

    def b1_step(i):
        h, k = i // 8 + 1, i % 8
        for side, d in enumerate((1, -1)):
            slot = at(d * (3 - h), b_order[k])
            if h == 2:
                add(b1, (1, k, d), slot)
            piece = part.b_half[side] if h == 1 else part.b
            send(b1, (h, k, d), slot, piece, place.along_y(d), "b")

    def a1_end(k):
        for d in (1, -1):
            add(a1, (4, k, d), at(a_order[k], 0))

    def b1_end(k):
        for d in (1, -1):
            add(b1, (2, k, d), at(0, b_order[k]))

    def a2_step(h):
        for side, d in enumerate((1, -1)):
            slot = at(d * (3 - h), 0)
            if h == 2:
                add(a2, (1, d), slot)
            send(a2, (h, d), slot, part.a_half[side] if h == 1 else part.a, place.along_y(d), "a")

    def b2_step(h):
        for side, d in enumerate((1, -1)):
            slot = at(0, d * (5 - h))
            if h > 1:
                add(b2, (h - 1, d), slot)
            send(b2, (h, d), slot, part.b_half[side] if h == 1 else part.b, place.along_z(d), "b")

    def end(book, key, piece):
        own = at(0, 0)
        for d in (1, -1):
            add(book, key + (d,), own)
        cols(result, own, piece)[...] = cols(part_sums, own, piece)[...]

    def step(i):
        if i < 16:
            a1_step(i)
        if 0 <= i - SHIFT < 16:
            b1_step(i - SHIFT)
        if 0 <= i - SHIFT - 10 < 8:
            b1_end(i - SHIFT - 10)
        if 0 <= i - 14 < 4:
            a1_end(i - 14)
        if i - SHIFT in (10, 12, 14, 16):
            b2_step((i - SHIFT - 8) // 2)
        if i in (14, 16):
            a2_step((i - 12) // 2)
        if i == 18:
            end(a2, (2,), part.a)
        if i - SHIFT == 18:
            end(b2, (4,), part.b)

    return [functools.partial(step, i) for i in range(19 + SHIFT)]


GATHER_WIRES = 4 + 8 + 32 + 32
SCATTER_WIRES = 32 + 32 + 4 + 8
OTHER_WIRES = 11 + 24 + 4
WIRES = GATHER_WIRES + SCATTER_WIRES + OTHER_WIRES


def column_block(c):
    return pl.ds(pl.multiple_of(c * BLOCK, BLOCK), BLOCK)


def block_pieces(body, begin, end, size):
    def piece(first, last):
        def run():
            @pl.loop(first, last)
            def _(c):
                body(column_block(c))

        return run

    return [piece(c, min(c + size, end)) for c in range(begin, end, size)]


def in_order(timed):
    for _, _, step in sorted((key, n, step) for n, (key, step) in enumerate(timed)):
        step()


def at_times(steps, begin, apart=1.0):
    return [(begin + apart * i, step) for i, step in enumerate(steps)]


def core(
    momentum, gradient, basis,
    coeffs, ortho, inverse, new_basis,
    q_all, w_part, w_all, land_a, land_b, m_buf, g_buf, b_high, b_low, c_buf,
    p_part, p_core, p_x, p_all, p_t, gram_own, gram_z, gram_y, work, linv, linv_high, linv_low, norm_sum, norm_core, norm_x,
    send, recv, local,
):
    place = Place()
    wires = Wires(send, recv)
    start = wires.range(GATHER_WIRES + SCATTER_WIRES, OTHER_WIRES)
    f, t, y, z, x, core_index = place.f, place.t, place.y, place.z, place.x, place.c

    loads = [
        pltpu.make_async_copy(basis, q_all.at[f], local.at[0]),
        pltpu.make_async_copy(momentum, m_buf, local.at[1]),
        pltpu.make_async_copy(gradient, g_buf, local.at[2]),
    ]
    for load in loads:
        load.start()

    barrier = pltpu.get_barrier_semaphore()
    peers = (
        [place.along_y(d) for d in range(1, Y)]
        + [place.along_z(d) for d in range(1, Z)]
        + [place.along_x(d) for d in range(1, 4)]
        + [place.other_core()]
    )
    for peer in peers:
        pl.semaphore_signal(barrier, inc=1, device_id=peer, device_id_type=MESH)
    pl.semaphore_wait(barrier, len(peers))

    def split_block(at):
        high, low = split(m_buf[:, at] + g_buf[:, at].astype(f32))
        b_high[:, at] = high
        b_low[:, at] = low

    def project(at):
        q = split(q_all[:, :, at].reshape(RANK, BLOCK))
        p_part[...] += dot3((b_high[:, at], b_low[:, at]), q, ((1,), (1,))).reshape(T, M // T, RANK)

    def loaded():
        p_part[...] = jnp.zeros_like(p_part)
        loads[1].wait()
        loads[2].wait()

    blocks = N // BLOCK
    loads[0].wait()
    timed = at_times(gather_steps(place, wires.range(0, GATHER_WIRES), q_all, PART), 0)
    timed += [(1.4, loaded)]
    timed += at_times(block_pieces(split_block, 0, blocks, 1), 1.5)
    in_order(timed)
    for piece in block_pieces(project, 0, blocks, blocks):
        piece()

    mine = 4 * core_index
    copy = start(p_part.at[pl.ds(4 - mine, 4)], p_core, place.other_core())
    copy.wait_recv()
    p_core[...] += p_part[pl.ds(mine, 4)]
    copies = [
        start(p_core.at[(x + d) % 4], p_x.at[x], place.along_x(d)) for d in (2, 1, 3)
    ]
    p_x[x] = p_core[x]
    for copy in copies:
        copy.wait_recv()
    p_all[mine + x] = (p_x[0] + p_x[1]) + (p_x[2] + p_x[3])

    def copy_p(block, to):
        return start(p_all.at[block], p_all.at[block], to)

    copies = [copy_p(mine + x, place.along_x(d)) for d in (2, 1, 3)]
    core_copies = [copy_p(mine + x, place.other_core())]
    for d, copy in ((1, copies[1]), (3, copies[2]), (2, copies[0])):
        copy.wait_recv()
        core_copies.append(copy_p(mine + (x - d + 4) % 4, place.other_core()))
    for copy in core_copies:
        copy.wait_recv()

    proj = p_all[...].reshape(M, RANK)
    p_t[...] = proj.T
    rows = p_t[pl.ds(pl.multiple_of(t * (RANK // T), RANK // T), RANK // T), :]
    own = exact(rows, proj)
    for j in range(Z):
        gram_own[j] = own[8 * (j // 2) : 8 * (j // 2) + 8, 128 * (j % 2) : 128 * (j % 2) + 128]
    gram_copies = [
        start(gram_own.at[(z + d) % Z], gram_z.at[z], place.along_z(d)) for d in range(1, Z)
    ]
    gram_sent = list(gram_copies)
    gram_z[z] = gram_own[z]

    pt_split = split(p_t[...])

    def coefficients(at):
        w_part[:, :, at] = dot3(pt_split, (b_high[:, at], b_low[:, at])).reshape(F, R, BLOCK)

    a_blocks = -(-PART.a[1] // BLOCK)
    for piece in block_pieces(coefficients, 0, a_blocks, a_blocks):
        piece()

    def summed(ref, count):
        total = ref[0]
        for i in range(1, count):
            total = total + ref[i]
        return total

    def arrived(*sent):
        for copy in gram_copies:
            copy.wait_recv()
        gram_copies.clear()

    def send_gram(copies):
        gram_copies.extend(copies)
        gram_sent.extend(copies)

    tile = (4 * t + z // 2, slice(None), pl.ds(pl.multiple_of(z % 2 * 128, 128), 128))

    def gram_rows(owner):
        return work.at[pl.ds(4 * owner, 4), :, pl.ds(0, RANK)]

    def to_other_core(owner):
        return start(gram_rows(owner), gram_rows(owner), place.other_core())

    def gram_1():
        arrived()
        gram_y[y] = summed(gram_z, Z)
        send_gram([start(gram_y.at[y], gram_y.at[y], place.along_y(d)) for d in range(1, Y)])

    def gram_2():
        arrived()
        work[tile] = summed(gram_y, Y)
        send_gram([start(work.at[tile], work.at[tile], place.along_z(d)) for d in range(1, Z)])

    def gram_3():
        arrived()
        send_gram([start(gram_rows(t), gram_rows(t), place.along_x(d)) for d in range(1, 4)])

    def gram_4():
        arrived()
        send_gram([to_other_core((x + d) % 4 * 2 + core_index) for d in range(4)])

    def gram_5():
        arrived()
        wires.drain(gram_sent)
        row = lax.broadcasted_iota(jnp.int32, (RANK, RANK), 0)
        lane = lax.broadcasted_iota(jnp.int32, (RANK, RANK), 1)
        work[:, :, RANK:] = jnp.where(row == lane, 1.0, 0.0).astype(f32).reshape(F, R, RANK)

    lane = lax.broadcasted_iota(jnp.int32, (NB, 128), 1)
    sub = lax.broadcasted_iota(jnp.int32, (NB, 128), 0)

    def panel(p):
        tiles = NB // R
        here = work[pl.ds(p * tiles, tiles)].reshape(NB, 2 * RANK)
        start = p * NB
        low_half = jnp.where(start < 128, here[:, :128], here[:, 128:256])
        block = pltpu.roll(low_half, (128 - start % 128) % 128, 1)
        columns = [jnp.broadcast_to(block[:, j : j + 1], (NB, 128)) for j in range(NB)]
        right = jnp.where(lane == sub, 1.0, 0.0).astype(f32)
        diag = jnp.ones((NB, 128), f32)
        for j in range(NB):
            pivot = jnp.broadcast_to(columns[j][j : j + 1, :], (NB, 128))
            diag = jnp.where(sub == j, pivot, diag)
            if j < NB - 1:
                factor = jnp.where(sub > j, columns[j] * (1.0 / pivot), 0.0)
                for i in range(j + 1, NB):
                    columns[i] = columns[i] - factor * columns[i][j : j + 1, :]
                right = right - factor * right[j : j + 1, :]
        right = right * lax.rsqrt(diag)
        done = right[:, 0:1] * here[0:1, :]
        for j in range(1, NB):
            done = done + right[:, j : j + 1] * here[j : j + 1, :]
        linv[pl.ds(p * tiles, tiles)] = done[:, RANK:].reshape(tiles, R, RANK)
        high = done.astype(bf16).astype(f32)
        mid = (done - high).astype(bf16).astype(f32)
        low = (done - high) - mid
        left = jnp.concatenate([v[:, :RANK] for v in (high, high, mid, high, low, mid)]).astype(bf16)
        beside = jnp.concatenate([high, mid, high, low, high, mid]).astype(bf16)
        work[...] -= dot(left, beside, ((0,), (0,))).reshape(F, R, 2 * RANK)

    def panels(begin, end):
        def run():
            @pl.loop(begin, end)
            def _(p):
                panel(p)

        return run

    def orthogonal():
        ortho[...] = exact(p_all[...].reshape(M, RANK), linv[...].reshape(RANK, RANK), ((1,), (1,)))
        linv_high[...], linv_low[...] = split(linv[...].reshape(RANK, RANK))
        norm_sum[...] = jnp.zeros_like(norm_sum)

    def multiply(at):
        part = dot3((linv_high[...], linv_low[...]), split(w_all[:, :, at].reshape(RANK, BLOCK)))
        c_buf[:, at] = part
        squares = part * part
        norm_sum[...] += squares[:, :128] + squares[:, 128:]

    lanes = wires.range(GATHER_WIRES, SCATTER_WIRES)
    steps = scatter_steps(place, lanes, w_part, w_all, land_a, land_b, PART)
    steps += gather_steps(place, wires.range(0, GATHER_WIRES), w_all, PART)
    timed = at_times(steps, 0)
    timed += at_times(block_pieces(coefficients, a_blocks, blocks, blocks), SHIFT - 0.9)
    timed += [(4.5, gram_1), (7.5, gram_2), (11.5, gram_3), (14.5, gram_4), (16.5, gram_5)]
    timed += at_times([panels(p, p + 2) for p in range(0, RANK // NB, 2)], 17.5)
    timed += [(26.5, orthogonal)]
    in_order(timed)

    stores = []
    for size, piece in zip((7, 6), block_pieces(multiply, 0, blocks, 7), strict=True):
        piece()
        at = pl.ds(len(stores) * 7 * BLOCK, size * BLOCK)
        stores.append(pltpu.make_async_copy(c_buf.at[:, at], coeffs.at[:, at], local.at[len(stores)]))
        stores[-1].start()
    own_norms = jnp.sum(norm_sum[...].T, axis=0, keepdims=True)
    norm_core[0, 0:8] = jnp.broadcast_to(own_norms[:, :128], (8, 128))
    norm_core[0, 8:16] = jnp.broadcast_to(own_norms[:, 128:], (8, 128))
    copy = start(norm_core.at[0], norm_core.at[1], place.other_core())
    copy.wait_recv()
    norm_x[x] = norm_core[0] + norm_core[1]
    copies = [start(norm_x.at[x], norm_x.at[x], place.along_x(d)) for d in (2, 1, 3)]
    for copy in copies:
        copy.wait_recv()
    scale = lax.rsqrt((norm_x[0] + norm_x[1]) + (norm_x[2] + norm_x[3]) + norm_eps)
    inverse_row = jnp.concatenate([scale[0:8], scale[8:16]], axis=1)
    inverse[...] = inverse_row
    lanes = lax.broadcasted_iota(jnp.int32, (R, RANK), 1)
    subs = lax.broadcasted_iota(jnp.int32, (R, RANK), 0)
    own_inverse = jnp.sum(jnp.where(lanes == subs + f * R, inverse_row, 0.0), axis=1, keepdims=True)
    new_basis[...] = c_buf[pl.ds(pl.multiple_of(f * R, R), R), :] * own_inverse
    for copy in stores:
        copy.wait()
    wires.drain()


def core_call(momentum, gradient, basis):
    any_space = pl.BlockSpec(memory_space=pl.ANY)
    vmem = pl.BlockSpec(memory_space=pltpu.VMEM)
    return pl.pallas_call(
        core,
        out_shape=(
            jax.ShapeDtypeStruct((RANK, N), f32),
            jax.ShapeDtypeStruct((M, RANK), f32),
            jax.ShapeDtypeStruct((8, RANK), f32),
            jax.ShapeDtypeStruct((R, N), f32),
        ),
        in_specs=[any_space] * 3,
        out_specs=(any_space, vmem, vmem, vmem),
        scratch_shapes=[
            pltpu.VMEM((F, R, N), f32),
            pltpu.VMEM((F, R, N), f32),
            pltpu.VMEM((F, R, N), f32),
            pltpu.VMEM((A_LANDS, R, PART.a[1]), f32),
            pltpu.VMEM((B_LANDS, R, PART.b[1]), f32),
            pltpu.VMEM((M, N), f32),
            pltpu.VMEM((M, N), bf16),
            pltpu.VMEM((M, N), bf16),
            pltpu.VMEM((M, N), bf16),
            pltpu.VMEM((RANK, N), f32),
            pltpu.VMEM((T, M // T, RANK), f32),
            pltpu.VMEM((T // 2, M // T, RANK), f32),
            pltpu.VMEM((T // 2, M // T, RANK), f32),
            pltpu.VMEM((T, M // T, RANK), f32),
            pltpu.VMEM((RANK, M), f32),
            pltpu.VMEM((Z, 8, 128), f32),
            pltpu.VMEM((Z, 8, 128), f32),
            pltpu.VMEM((Y, 8, 128), f32),
            pltpu.VMEM((F, R, 2 * RANK), f32),
            pltpu.VMEM((F, R, RANK), f32),
            pltpu.VMEM((RANK, RANK), bf16),
            pltpu.VMEM((RANK, RANK), bf16),
            pltpu.VMEM((RANK, 128), f32),
            pltpu.VMEM((2, 16, 128), f32),
            pltpu.VMEM((4, 16, 128), f32),
            pltpu.SemaphoreType.DMA((POOL,)),
            pltpu.SemaphoreType.DMA((WIRES,)),
            pltpu.SemaphoreType.DMA((3,)),
        ],
        compiler_params=pltpu.CompilerParams(
            collective_id=0, has_side_effects=True, vmem_limit_bytes=60 * 2**20
        ),
        name="core",
    )(momentum, gradient, basis)


def update(momentum, gradient, coeffs, ortho, inverse, new_momentum, step):
    buffer = momentum[...] + gradient[...].astype(f32)
    high, low = split(coeffs[...])
    basis = ortho[...]
    new_momentum[...] = buffer - (1.0 - momentum_decay) * dot(basis.astype(bf16), high)
    scale = (ROWS * COLS / RANK) ** 0.5
    scaled = split(basis * (inverse[0:1, :] * scale))
    step[...] = dot3(scaled, (high, low)).astype(bf16)


def update_call(momentum, gradient, coeffs, ortho, inverse):
    wide = N // 2

    def block(rows):
        return pl.BlockSpec((rows, wide), lambda c: (0, c))

    return pl.pallas_call(
        update,
        grid=(N // wide,),
        out_shape=(jax.ShapeDtypeStruct((M, N), f32), jax.ShapeDtypeStruct((M, N), bf16)),
        in_specs=[
            block(M), block(M), block(RANK),
            pl.BlockSpec((M, RANK), lambda c: (0, 0)),
            pl.BlockSpec((8, RANK), lambda c: (0, 0)),
        ],
        out_specs=(block(M), block(M)),
        compiler_params=pltpu.CompilerParams(vmem_limit_bytes=60 * 2**20),
        name="update",
    )(momentum, gradient, coeffs, ortho, inverse)


def on_device(momentum, gradient, basis):
    coeffs, ortho, inverse, new_basis = core_call(momentum, gradient, basis)
    new_momentum, step = update_call(momentum, gradient, coeffs, ortho, inverse)
    return (new_momentum, new_basis, step)


def solution(mesh):
    placed = (P("fsdp", "tp"), P("fsdp", "tp"), P("fsdp", "tp"))
    return jax.shard_map(
        on_device,
        mesh=mesh,
        in_specs=placed,
        out_specs=(P("fsdp", "tp"), P("fsdp", "tp"), P("fsdp", "tp")),
        check_vma=False,
    )
```

```python
import functools

import jax
import jax.numpy as jnp
from jax import lax
from jax.experimental import pallas as pl
from jax.experimental.pallas import tpu as pltpu
from jax.sharding import PartitionSpec as P

ROWS = 8192
COLS = 26624
RANK = 256

momentum_decay = 0.95
norm_eps = 1e-06

Y, Z, T = 4, 8, 8
F = Y * Z
M = ROWS // F
N = COLS // T
R = RANK // F
BLOCK = 256
NB = 16


class Part:
    def __init__(self, begin, size, cut):
        self.begin, self.size = begin, size
        self.a, self.b = (begin, cut), (begin + cut, size - cut)
        self.a_half, self.b_half = self.halves(self.a), self.halves(self.b)

    @staticmethod
    def halves(part):
        first = (part[1] // 128 + 1) // 2 * 128
        return (part[0], first), (part[0] + first, part[1] - first)


PARTS = (Part(0, N, 2432), Part(0, N, 0))
A_LANDS = 4 * 4 * 2 + 2 * 2
B_LANDS = 2 * 8 * 2 + 4 * 2
POOL = 32
OTHER_POOL = 16
EARLY = 7

MESH = pl.DeviceIdType.MESH
f32, bf16 = jnp.float32, jnp.bfloat16


def split(value):
    high = value.astype(bf16)
    return high, (value - high.astype(f32)).astype(bf16)


def dot(left, right, dims=((1,), (0,))):
    return lax.dot_general(left, right, (dims, ((), ())), preferred_element_type=f32)


def dot3(left, right, dims=((1,), (0,))):
    (lh, ll), (rh, rl) = left, right
    return dot(lh, rh, dims) + (dot(lh, rl, dims) + dot(ll, rh, dims))


def exact(left, right, dims=((1,), (0,))):
    return lax.dot_general(
        left, right, (dims, ((), ())), precision=lax.Precision.HIGHEST, preferred_element_type=f32
    )


class Copy:
    def __init__(self, make):
        self.make, self.sent = make, False

    def start(self):
        self.make().start()

    def wait_recv(self):
        self.make().wait_recv()

    def wait_send(self):
        if not self.sent:
            self.make().wait_send()
        self.sent = True


class Wires:
    def __init__(self, send, recv, first, size):
        self.send, self.recv, self.first, self.size = send, recv, first, size
        self.last, self.used = {}, 0

    def range(self, begin, count):
        indices = iter(range(begin, begin + count))
        return lambda src, dst, to: self.start(src, dst, to, next(indices))

    def start(self, src, dst, to, index):
        place = self.first + self.used % self.size
        self.used += 1
        if place in self.last:
            self.last[place].wait_send()
        copy = Copy(
            lambda: pltpu.make_async_remote_copy(
                src_ref=src(),
                dst_ref=dst(),
                send_sem=self.send.at[place],
                recv_sem=self.recv.at[index],
                device_id=to,
                device_id_type=MESH,
            )
        )
        copy.start()
        self.last[place] = copy
        return copy

    def drain(self):
        for copy in self.last.values():
            copy.wait_send()


class Place:
    def __init__(self):
        self.f = lax.axis_index("fsdp")
        self.t = lax.axis_index("tp")
        self.y, self.z = self.f // Z, self.f % Z
        self.x, self.c = self.t // 2, self.t % 2
        self.slots = {
            (dy, dz): (self.y + dy) % Y * Z + (self.z + dz) % Z for dy in range(Y) for dz in range(Z)
        }

    def slot(self, dy, dz):
        return self.slots[dy % Y, dz % Z]

    def along_y(self, d):
        return {"fsdp": self.slot(d, 0)}

    def along_z(self, d):
        return {"fsdp": self.slot(0, d)}

    def along_x(self, d):
        return {"tp": (self.x + d) % 4 * 2 + self.c}

    def other_core(self):
        return {"tp": self.x * 2 + 1 - self.c}


def cols(ref, slot, part):
    return ref.at[slot, :, pl.ds(part[0], part[1])]


SIDES = ((0, 1), (1, -1))
A_ORDER = [(h, k) for h in range(1, 5) for k in range(4)]


def gather_steps(place, start, buf, part):
    a1, b1, a2, b2 = {}, {}, {}, {}
    a_slots = (0, -1, 1, 2)
    b_slots = (0, -1, 1, -2, 2, -3, 3, 4)
    b_order = [(1, k) for k in range(5)]
    b_order += [(2, 0), (1, 5), (2, 1), (1, 6), (2, 2), (1, 7)] + [(2, k) for k in range(3, 8)]
    at = place.slot

    def send(book, key, slot, piece, to):
        def here():
            return cols(buf, slot, piece)

        book[key] = start(here, here, to)

    def a1_step(k):
        if k == 0:
            for d in (2, 1, -1):
                send(a1, d, at(0, 0), part.a, place.along_y(d))
        else:
            a1[-a_slots[k] if k < 3 else 2].wait_recv()

    def a2_step(h, k):
        for side, d in SIDES:
            if h > 1:
                a2[h - 1, k, d].wait_recv()
            piece = part.a_half[side] if h == 4 else part.a
            send(a2, (h, k, d), at(a_slots[k], -d * (h - 1)), piece, place.along_z(d))

    def b1_step(k):
        if k == 0:
            for d in (2, -2, 1, -1):
                send(b1, d, at(0, 0), part.b, place.along_z(d))
        elif k < 7:
            b1[-b_slots[k]].wait_recv()
            if k in (3, 4):
                side, d = SIDES[k - 3]
                send(b1, 4 * d, at(0, -2 * d), part.b_half[side], place.along_z(2 * d))
                send(b1, 3 * d, at(0, -2 * d), part.b, place.along_z(d))
        else:
            b1[4].wait_recv()
            b1[-4].wait_recv()

    def b2_step(h, k):
        for side, d in SIDES:
            if h == 2:
                b2[1, k, d].wait_recv()
            piece = part.b_half[side] if h == 2 else part.b
            send(b2, (h, k, d), at(-d * (h - 1), b_slots[k]), piece, place.along_y(d))

    def step(i):
        for order, width, first, second in (
            (b_order, part.b[1], b1_step, b2_step),
            (A_ORDER, part.a[1], a1_step, a2_step),
        ):
            if width:
                h, k = order[i]
                if h == 1:
                    first(k)
                second(h, k)

    def last():
        for book, h, slots in ((a2, 4, a_slots), (b2, 2, b_slots)):
            if book:
                for k in range(len(slots)):
                    for _, d in SIDES:
                        book[h, k, d].wait_recv()

    return [functools.partial(step, i) for i in range(16)] + [last]


def scatter_steps(place, start, part_sums, result, land_a, land_b, part):
    a1, b1, a2, b2 = {}, {}, {}, {}
    a_slots = (2, 1, -1, 0)
    b_slots = (4, 3, -3, 2, -2, 1, -1, 0)
    b_order = [(1, k) for k in range(4)]
    b_order += [(2, 0), (1, 4), (2, 1), (1, 5), (2, 2), (1, 6), (2, 3), (1, 7)] + [(2, k) for k in range(4, 8)]
    at = place.slot
    used = {"a": {}, "b": {}}

    def send(book, key, slot, piece, to, kind):
        land = land_a if kind == "a" else land_b
        offset = piece[0] - (part.a if kind == "a" else part.b)[0]
        index = used[kind].setdefault(key, len(used[kind]))

        def there():
            return land.at[index, :, pl.ds(offset, piece[1])]

        book[key] = (start(lambda: cols(part_sums, slot, piece), there, to), there, piece)

    def add(book, key, slot):
        copy, there, piece = book[key]
        copy.wait_recv()
        own = cols(part_sums, slot, piece)
        own[...] += there()[...]

    def a1_step(h, k, sides=SIDES):
        for side, d in sides:
            slot = at(a_slots[k], d * (5 - h))
            if h > 1:
                add(a1, (h - 1, k, d), slot)
            piece = part.a_half[side] if h == 1 else part.a
            send(a1, (h, k, d), slot, piece, place.along_z(d), "a")

    def b1_step(h, k, sides=SIDES):
        for side, d in sides:
            slot = at(d * (3 - h), b_slots[k])
            if h == 2:
                add(b1, (1, k, d), slot)
            piece = part.b_half[side] if h == 1 else part.b
            send(b1, (h, k, d), slot, piece, place.along_y(d), "b")

    def a1_end(k):
        for _, d in SIDES:
            add(a1, (4, k, d), at(a_slots[k], 0))

    def b1_end(k):
        for _, d in SIDES:
            add(b1, (2, k, d), at(0, b_slots[k]))

    def a2_step(k):
        d = a_slots[k]
        send(a2, d, at(d, 0), part.a, place.along_y(d), "a")

    def b2_step(k):
        d = b_slots[k]
        if d == 4:
            for side, way in SIDES:
                send(b2, 4 * way, at(0, 4), part.b_half[side], place.along_z(2 * way), "b")
            return
        if abs(d) == 2:
            add(b2, 2 * d, at(0, d))
            add(b2, 3 * d // 2, at(0, d))
        send(b2, d, at(0, d), part.b, place.along_z(d // 3 if abs(d) == 3 else d), "b")

    def end(book, keys, piece):
        own = at(0, 0)
        for key in keys:
            add(book, key, own)
        cols(result, own, piece)[...] = cols(part_sums, own, piece)[...]

    early = SIDES[:1]

    def before():
        for k in range(4):
            if part.a[1]:
                a1_step(1, k, early)
            else:
                b1_step(1, k, early)

    def step(i):
        if i < 16:
            late = SIDES[1:] if i < 4 else SIDES
            if part.b[1]:
                b1_step(*b_order[i], SIDES if part.a[1] else late)
            if part.a[1]:
                a1_step(*A_ORDER[i], late)
        for k in range(8):
            if part.b[1] and i == b_order.index((2, k)) + 2:
                b1_end(k)
                if k < 7:
                    b2_step(k)
        for k in range(4):
            if part.a[1] and i == A_ORDER.index((4, k)) + 2:
                a1_end(k)
                if k < 3:
                    a2_step(k)
        if i == 19:
            if part.b[1]:
                end(b2, (2, -2, 1, -1), part.b)
            if part.a[1]:
                end(a2, (2, 1, -1), part.a)

    return [before], [functools.partial(step, i) for i in range(20)]


GATHER_WIRES = 3 + 8 + 32 + 32
SCATTER_WIRES = 32 + 32 + 3 + 8
OTHER_WIRES = 11 + 24 + 4
WIRES = GATHER_WIRES + SCATTER_WIRES + OTHER_WIRES


def column_block(c):
    return pl.ds(pl.multiple_of(c * BLOCK, BLOCK), BLOCK)


def block_pieces(body, begin, end, size):
    def piece(first, last):
        def run():
            @pl.loop(first, last, unroll=last - first)
            def _(c):
                body(column_block(c))

        return run

    return [piece(c, min(c + size, end)) for c in range(begin, end, size)]


def in_order(timed):
    for _, _, step in sorted((key, n, step) for n, (key, step) in enumerate(timed)):
        step()


def at_times(steps, begin, apart=1.0):
    return [(begin + apart * i, step) for i, step in enumerate(steps)]


def core(
    momentum, gradient, basis,
    coeffs, ortho, inverse, new_basis,
    q_all, w_part, w_all, land_a, land_b, m_buf, g_buf, b_high, b_low, c_buf,
    p_part, p_core, p_x, p_all, p_t, gram_own, gram_z, gram_y, work, linv, linv_high, linv_low, norm_sum, norm_core, norm_x,
    send, recv, local,
):
    place = Place()
    wires = Wires(send, recv, POOL, OTHER_POOL)
    core_wires = [Wires(send, recv, 0, POOL) for _ in PARTS]
    other_start = wires.range(GATHER_WIRES + SCATTER_WIRES, OTHER_WIRES)

    def start(src, dst, to):
        return other_start(lambda: src, lambda: dst, to)

    def by_core(lists):
        def both(steps):
            def run():
                for index, step in enumerate(steps):
                    pl.when(core_index == index)(step)

            return run

        return [both(steps) for steps in zip(*lists, strict=True)]

    def gather(buf):
        return by_core(
            [gather_steps(place, w.range(0, GATHER_WIRES), buf, part) for w, part in zip(core_wires, PARTS)]
        )
    f, t, y, z, x, core_index = place.f, place.t, place.y, place.z, place.x, place.c

    loads = [
        pltpu.make_async_copy(basis, q_all.at[f], local.at[0]),
        pltpu.make_async_copy(momentum, m_buf, local.at[1]),
        pltpu.make_async_copy(gradient, g_buf, local.at[2]),
    ]
    for load in loads:
        load.start()

    barrier = pltpu.get_barrier_semaphore()
    peers = (
        [place.along_y(d) for d in range(1, Y)]
        + [place.along_z(d) for d in range(1, Z)]
        + [place.along_x(d) for d in range(1, 4)]
        + [place.other_core()]
    )
    for peer in peers:
        pl.semaphore_signal(barrier, inc=1, device_id=peer, device_id_type=MESH)
    pl.semaphore_wait(barrier, len(peers))

    def split_block(at):
        high, low = split(m_buf[:, at] + g_buf[:, at].astype(f32))
        b_high[:, at] = high
        b_low[:, at] = low

    def project(at):
        q = split(q_all[:, :, at].reshape(RANK, BLOCK))
        p_part[...] += dot3((b_high[:, at], b_low[:, at]), q, ((1,), (1,))).reshape(T, M // T, RANK)

    def loaded():
        p_part[...] = jnp.zeros_like(p_part)
        loads[1].wait()
        loads[2].wait()

    blocks = N // BLOCK
    loads[0].wait()
    timed = at_times(gather(q_all), 0)
    timed += [(1.4, loaded)]
    timed += at_times(block_pieces(split_block, 0, blocks, 1), 1.5)
    in_order(timed)
    for piece in block_pieces(project, 0, blocks, blocks):
        piece()

    mine = 4 * core_index
    copy = start(p_part.at[pl.ds(4 - mine, 4)], p_core, place.other_core())
    copy.wait_recv()
    p_core[...] += p_part[pl.ds(mine, 4)]
    copies = [
        start(p_core.at[(x + d) % 4], p_x.at[x], place.along_x(d)) for d in (2, 1, 3)
    ]
    p_x[x] = p_core[x]
    for copy in copies:
        copy.wait_recv()
    p_all[mine + x] = (p_x[0] + p_x[1]) + (p_x[2] + p_x[3])

    def copy_p(block, to):
        return start(p_all.at[block], p_all.at[block], to)

    copies = [copy_p(mine + x, place.along_x(d)) for d in (2, 1, 3)]
    core_copies = [copy_p(mine + x, place.other_core())]
    for d, copy in ((1, copies[1]), (3, copies[2]), (2, copies[0])):
        copy.wait_recv()
        core_copies.append(copy_p(mine + (x - d + 4) % 4, place.other_core()))
    for copy in core_copies:
        copy.wait_recv()

    proj = p_all[...].reshape(M, RANK)
    p_t[...] = proj.T
    rows = p_t[pl.ds(pl.multiple_of(t * (RANK // T), RANK // T), RANK // T), :]
    own = exact(rows, proj)
    for j in range(Z):
        gram_own[j] = own[8 * (j // 2) : 8 * (j // 2) + 8, 128 * (j % 2) : 128 * (j % 2) + 128]
    gram_copies = [
        start(gram_own.at[(z + d) % Z], gram_z.at[z], place.along_z(d)) for d in range(1, Z)
    ]
    gram_sent = list(gram_copies)
    gram_z[z] = gram_own[z]

    pt_split = split(p_t[...])

    def coefficients(at):
        w_part[:, :, at] = dot3(pt_split, (b_high[:, at], b_low[:, at])).reshape(F, R, BLOCK)

    scatters = [
        scatter_steps(place, w.range(GATHER_WIRES, SCATTER_WIRES), w_part, w_all, land_a, land_b, part)
        for w, part in zip(core_wires, PARTS)
    ]
    before, after = (by_core(lists) for lists in zip(*scatters))
    (early,) = block_pieces(coefficients, 0, EARLY, EARLY)
    (late,) = block_pieces(coefficients, EARLY, blocks, blocks)
    early()
    before[0]()
    late()

    def summed(ref, count):
        total = ref[0]
        for i in range(1, count):
            total = total + ref[i]
        return total

    def arrived(*sent):
        for copy in gram_copies:
            copy.wait_recv()
        gram_copies.clear()

    def send_gram(copies):
        gram_copies.extend(copies)
        gram_sent.extend(copies)

    tile = (4 * t + z // 2, slice(None), pl.ds(pl.multiple_of(z % 2 * 128, 128), 128))

    def gram_rows(owner):
        return work.at[pl.ds(4 * owner, 4), :, pl.ds(0, RANK)]

    def to_other_core(owner):
        return start(gram_rows(owner), gram_rows(owner), place.other_core())

    def gram_1():
        arrived()
        gram_y[y] = summed(gram_z, Z)
        send_gram([start(gram_y.at[y], gram_y.at[y], place.along_y(d)) for d in range(1, Y)])

    def gram_2():
        arrived()
        work[tile] = summed(gram_y, Y)
        send_gram([start(work.at[tile], work.at[tile], place.along_z(d)) for d in range(1, Z)])

    def gram_3():
        arrived()
        send_gram([start(gram_rows(t), gram_rows(t), place.along_x(d)) for d in range(1, 4)])

    def gram_4():
        arrived()
        send_gram([to_other_core((x + d) % 4 * 2 + core_index) for d in range(4)])

    def gram_5():
        arrived()
        for copy in gram_sent:
            copy.wait_send()
        row = lax.broadcasted_iota(jnp.int32, (RANK, RANK), 0)
        lane = lax.broadcasted_iota(jnp.int32, (RANK, RANK), 1)
        work[:, :, RANK:] = jnp.where(row == lane, 1.0, 0.0).astype(f32).reshape(F, R, RANK)

    lane = lax.broadcasted_iota(jnp.int32, (NB, 128), 1)
    sub = lax.broadcasted_iota(jnp.int32, (NB, 128), 0)

    def panel(p):
        tiles = NB // R
        here = work[pl.ds(p * tiles, tiles)].reshape(NB, 2 * RANK)
        start = p * NB
        low_half = jnp.where(start < 128, here[:, :128], here[:, 128:256])
        block = pltpu.roll(low_half, (128 - start % 128) % 128, 1)
        columns = [jnp.broadcast_to(block[:, j : j + 1], (NB, 128)) for j in range(NB)]
        right = jnp.where(lane == sub, 1.0, 0.0).astype(f32)
        diag = jnp.ones((NB, 128), f32)
        for j in range(NB):
            pivot = jnp.broadcast_to(columns[j][j : j + 1, :], (NB, 128))
            diag = jnp.where(sub == j, pivot, diag)
            if j < NB - 1:
                factor = jnp.where(sub > j, columns[j] * (1.0 / pivot), 0.0)
                for i in range(j + 1, NB):
                    columns[i] = columns[i] - factor * columns[i][j : j + 1, :]
                right = right - factor * right[j : j + 1, :]
        right = right * lax.rsqrt(diag)
        done = right[:, 0:1] * here[0:1, :]
        for j in range(1, NB):
            done = done + right[:, j : j + 1] * here[j : j + 1, :]
        linv[pl.ds(p * tiles, tiles)] = done[:, RANK:].reshape(tiles, R, RANK)
        high = done.astype(bf16).astype(f32)
        mid = (done - high).astype(bf16).astype(f32)
        low = (done - high) - mid
        left = jnp.concatenate([v[:, :RANK] for v in (high, high, mid, high, low, mid)]).astype(bf16)
        beside = jnp.concatenate([high, mid, high, low, high, mid]).astype(bf16)
        work[...] -= dot(left, beside, ((0,), (0,))).reshape(F, R, 2 * RANK)

    def panels(begin, end):
        def run():
            @pl.loop(begin, end)
            def _(p):
                panel(p)

        return run

    def orthogonal():
        ortho[...] = exact(p_all[...].reshape(M, RANK), linv[...].reshape(RANK, RANK), ((1,), (1,)))
        linv_high[...], linv_low[...] = split(linv[...].reshape(RANK, RANK))
        norm_sum[...] = jnp.zeros_like(norm_sum)

    def multiply(at):
        part = dot3((linv_high[...], linv_low[...]), split(w_all[:, :, at].reshape(RANK, BLOCK)))
        c_buf[:, at] = part
        squares = part * part
        norm_sum[...] += squares[:, :128] + squares[:, 128:]

    timed = at_times(after + gather(w_all), 0)
    timed += [(5.5, gram_1), (8.5, gram_2), (12.5, gram_3), (15.5, gram_4), (17.5, gram_5)]
    timed += at_times([panels(p, p + 1) for p in range(RANK // NB)], 18.5)
    timed += [(35.5, orthogonal)]
    in_order(timed)

    stores = []
    for size, piece in zip((7, 6), block_pieces(multiply, 0, blocks, 7), strict=True):
        piece()
        at = pl.ds(len(stores) * 7 * BLOCK, size * BLOCK)
        stores.append(pltpu.make_async_copy(c_buf.at[:, at], coeffs.at[:, at], local.at[len(stores)]))
        stores[-1].start()
    own_norms = jnp.sum(norm_sum[...].T, axis=0, keepdims=True)
    norm_core[0, 0:8] = jnp.broadcast_to(own_norms[:, :128], (8, 128))
    norm_core[0, 8:16] = jnp.broadcast_to(own_norms[:, 128:], (8, 128))
    copy = start(norm_core.at[0], norm_core.at[1], place.other_core())
    copy.wait_recv()
    norm_x[x] = norm_core[0] + norm_core[1]
    copies = [start(norm_x.at[x], norm_x.at[x], place.along_x(d)) for d in (2, 1, 3)]
    for copy in copies:
        copy.wait_recv()
    scale = lax.rsqrt((norm_x[0] + norm_x[1]) + (norm_x[2] + norm_x[3]) + norm_eps)
    inverse_row = jnp.concatenate([scale[0:8], scale[8:16]], axis=1)
    inverse[...] = inverse_row
    lanes = lax.broadcasted_iota(jnp.int32, (R, RANK), 1)
    subs = lax.broadcasted_iota(jnp.int32, (R, RANK), 0)
    own_inverse = jnp.sum(jnp.where(lanes == subs + f * R, inverse_row, 0.0), axis=1, keepdims=True)
    new_basis[...] = c_buf[pl.ds(pl.multiple_of(f * R, R), R), :] * own_inverse
    for copy in stores:
        copy.wait()
    wires.drain()
    by_core([[w.drain] for w in core_wires])[0]()


def core_call(momentum, gradient, basis):
    any_space = pl.BlockSpec(memory_space=pl.ANY)
    vmem = pl.BlockSpec(memory_space=pltpu.VMEM)
    return pl.pallas_call(
        core,
        out_shape=(
            jax.ShapeDtypeStruct((RANK, N), f32),
            jax.ShapeDtypeStruct((M, RANK), f32),
            jax.ShapeDtypeStruct((8, RANK), f32),
            jax.ShapeDtypeStruct((R, N), f32),
        ),
        in_specs=[any_space] * 3,
        out_specs=(any_space, vmem, vmem, vmem),
        scratch_shapes=[
            pltpu.VMEM((F, R, N), f32),
            pltpu.VMEM((F, R, N), f32),
            pltpu.VMEM((F, R, N), f32),
            pltpu.VMEM((A_LANDS, R, max(part.a[1] for part in PARTS)), f32),
            pltpu.VMEM((B_LANDS, R, max(part.b[1] for part in PARTS)), f32),
            pltpu.VMEM((M, N), f32),
            pltpu.VMEM((M, N), bf16),
            pltpu.VMEM((M, N), bf16),
            pltpu.VMEM((M, N), bf16),
            pltpu.VMEM((RANK, N), f32),
            pltpu.VMEM((T, M // T, RANK), f32),
            pltpu.VMEM((T // 2, M // T, RANK), f32),
            pltpu.VMEM((T // 2, M // T, RANK), f32),
            pltpu.VMEM((T, M // T, RANK), f32),
            pltpu.VMEM((RANK, M), f32),
            pltpu.VMEM((Z, 8, 128), f32),
            pltpu.VMEM((Z, 8, 128), f32),
            pltpu.VMEM((Y, 8, 128), f32),
            pltpu.VMEM((F, R, 2 * RANK), f32),
            pltpu.VMEM((F, R, RANK), f32),
            pltpu.VMEM((RANK, RANK), bf16),
            pltpu.VMEM((RANK, RANK), bf16),
            pltpu.VMEM((RANK, 128), f32),
            pltpu.VMEM((2, 16, 128), f32),
            pltpu.VMEM((4, 16, 128), f32),
            pltpu.SemaphoreType.DMA((POOL + OTHER_POOL,)),
            pltpu.SemaphoreType.DMA((WIRES,)),
            pltpu.SemaphoreType.DMA((3,)),
        ],
        compiler_params=pltpu.CompilerParams(
            collective_id=0, has_side_effects=True, vmem_limit_bytes=60 * 2**20
        ),
        name="core",
    )(momentum, gradient, basis)


def update(momentum, gradient, coeffs, ortho, inverse, own_basis, new_momentum, step, new_basis):
    new_basis[...] = own_basis[...]
    buffer = momentum[...] + gradient[...].astype(f32)
    high, low = split(coeffs[...])
    basis = ortho[...]
    new_momentum[...] = buffer - (1.0 - momentum_decay) * dot(basis.astype(bf16), high)
    scale = (ROWS * COLS / RANK) ** 0.5
    scaled = split(basis * (inverse[0:1, :] * scale))
    step[...] = dot3(scaled, (high, low)).astype(bf16)


def update_call(momentum, gradient, coeffs, ortho, inverse, own_basis):
    wide = N // 2

    def block(rows):
        return pl.BlockSpec((rows, wide), lambda c: (0, c))

    return pl.pallas_call(
        update,
        grid=(N // wide,),
        out_shape=(
            jax.ShapeDtypeStruct((M, N), f32),
            jax.ShapeDtypeStruct((M, N), bf16),
            jax.ShapeDtypeStruct((R, N), f32),
        ),
        in_specs=[
            block(M), block(M), block(RANK),
            pl.BlockSpec((M, RANK), lambda c: (0, 0)),
            pl.BlockSpec((8, RANK), lambda c: (0, 0)),
            block(R),
        ],
        out_specs=(block(M), block(M), block(R)),
        compiler_params=pltpu.CompilerParams(vmem_limit_bytes=60 * 2**20),
        name="update",
    )(momentum, gradient, coeffs, ortho, inverse, own_basis)


def on_device(momentum, gradient, basis):
    coeffs, ortho, inverse, own_basis = core_call(momentum, gradient, basis)
    new_momentum, step, new_basis = update_call(momentum, gradient, coeffs, ortho, inverse, own_basis)
    return (new_momentum, new_basis, step)


def solution(mesh):
    placed = (P("fsdp", "tp"), P("fsdp", "tp"), P("fsdp", "tp"))
    return jax.shard_map(
        on_device,
        mesh=mesh,
        in_specs=placed,
        out_specs=(P("fsdp", "tp"), P("fsdp", "tp"), P("fsdp", "tp")),
        check_vma=False,
    )
```

```python
import functools

import jax
import jax.numpy as jnp
from jax import lax
from jax.experimental import pallas as pl
from jax.experimental.pallas import tpu as pltpu
from jax.sharding import PartitionSpec as P

ROWS = 8192
COLS = 26624
RANK = 256

momentum_decay = 0.95
norm_eps = 1e-06

Y, Z, T = 4, 8, 8
F = Y * Z
M = ROWS // F
N = COLS // T
R = RANK // F
BLOCK = 256
NB = 16


class Part:
    def __init__(self, begin, size, cut):
        self.begin, self.size = begin, size
        self.a, self.b = (begin, cut), (begin + cut, size - cut)
        self.a_half, self.b_half = self.halves(self.a), self.halves(self.b)

    @staticmethod
    def halves(part):
        first = (part[1] // 128 + 1) // 2 * 128
        return (part[0], first), (part[0] + first, part[1] - first)


PARTS = (Part(0, N, 2432), Part(0, N, 0))
A_LANDS = 4 * 4 * 2 + 2 * 2
B_LANDS = 2 * 8 * 2 + 4 * 2
POOL = 32
OTHER_POOL = 16
EARLY = 7

MESH = pl.DeviceIdType.MESH
f32, bf16 = jnp.float32, jnp.bfloat16


def split(value):
    high = value.astype(bf16)
    return high, (value - high.astype(f32)).astype(bf16)


def dot(left, right, dims=((1,), (0,))):
    return lax.dot_general(left, right, (dims, ((), ())), preferred_element_type=f32)


def dot3(left, right, dims=((1,), (0,))):
    (lh, ll), (rh, rl) = left, right
    return dot(lh, rh, dims) + (dot(lh, rl, dims) + dot(ll, rh, dims))


def exact(left, right, dims=((1,), (0,))):
    return lax.dot_general(
        left, right, (dims, ((), ())), precision=lax.Precision.HIGHEST, preferred_element_type=f32
    )


class Copy:
    def __init__(self, make):
        self.make, self.sent = make, False

    def start(self):
        self.make().start()

    def wait_recv(self):
        self.make().wait_recv()

    def wait_send(self):
        if not self.sent:
            self.make().wait_send()
        self.sent = True


class Wires:
    def __init__(self, send, recv, first, size):
        self.send, self.recv, self.first, self.size = send, recv, first, size
        self.last, self.used = {}, 0

    def range(self, begin, count):
        indices = iter(range(begin, begin + count))
        return lambda src, dst, to: self.start(src, dst, to, next(indices))

    def start(self, src, dst, to, index):
        place = self.first + self.used % self.size
        self.used += 1
        if place in self.last:
            self.last[place].wait_send()
        copy = Copy(
            lambda: pltpu.make_async_remote_copy(
                src_ref=src(),
                dst_ref=dst(),
                send_sem=self.send.at[place],
                recv_sem=self.recv.at[index],
                device_id=to,
                device_id_type=MESH,
            )
        )
        copy.start()
        self.last[place] = copy
        return copy

    def drain(self):
        for copy in self.last.values():
            copy.wait_send()


class Place:
    def __init__(self):
        self.f = lax.axis_index("fsdp")
        self.t = lax.axis_index("tp")
        self.y, self.z = self.f // Z, self.f % Z
        self.x, self.c = self.t // 2, self.t % 2
        self.slots = {
            (dy, dz): (self.y + dy) % Y * Z + (self.z + dz) % Z for dy in range(Y) for dz in range(Z)
        }

    def slot(self, dy, dz):
        return self.slots[dy % Y, dz % Z]

    def along_y(self, d):
        return {"fsdp": self.slot(d, 0)}

    def along_z(self, d):
        return {"fsdp": self.slot(0, d)}

    def along_x(self, d):
        return {"tp": (self.x + d) % 4 * 2 + self.c}

    def other_core(self):
        return {"tp": self.x * 2 + 1 - self.c}


def cols(ref, slot, part):
    return ref.at[slot, :, pl.ds(part[0], part[1])]


SIDES = ((0, 1), (1, -1))
A_ORDER = [(h, k) for h in range(1, 5) for k in range(4)]


def gather_steps(place, start, buf, part):
    a1, b1, a2, b2 = {}, {}, {}, {}
    a_slots = (0, -1, 1, 2)
    b_slots = (0, -1, 1, -2, 2, -3, 3, 4)
    b_order = [(1, k) for k in range(5)]
    b_order += [(2, 0), (1, 5), (2, 1), (1, 6), (2, 2), (1, 7)] + [(2, k) for k in range(3, 8)]
    at = place.slot

    def send(book, key, slot, piece, to):
        def here():
            return cols(buf, slot, piece)

        book[key] = start(here, here, to)

    def a1_step(k):
        if k == 0:
            for d in (2, 1, -1):
                send(a1, d, at(0, 0), part.a, place.along_y(d))
        else:
            a1[-a_slots[k] if k < 3 else 2].wait_recv()

    def a2_step(h, k):
        for side, d in SIDES:
            if h > 1:
                a2[h - 1, k, d].wait_recv()
            piece = part.a_half[side] if h == 4 else part.a
            send(a2, (h, k, d), at(a_slots[k], -d * (h - 1)), piece, place.along_z(d))

    def b1_step(k):
        if k == 0:
            for d in (2, -2, 1, -1):
                send(b1, d, at(0, 0), part.b, place.along_z(d))
        elif k < 7:
            b1[-b_slots[k]].wait_recv()
            if k in (3, 4):
                side, d = SIDES[k - 3]
                send(b1, 4 * d, at(0, -2 * d), part.b_half[side], place.along_z(2 * d))
                send(b1, 3 * d, at(0, -2 * d), part.b, place.along_z(d))
        else:
            b1[4].wait_recv()
            b1[-4].wait_recv()

    def b2_step(h, k):
        for side, d in SIDES:
            if h == 2:
                b2[1, k, d].wait_recv()
            piece = part.b_half[side] if h == 2 else part.b
            send(b2, (h, k, d), at(-d * (h - 1), b_slots[k]), piece, place.along_y(d))

    def step(i):
        for order, width, first, second in (
            (b_order, part.b[1], b1_step, b2_step),
            (A_ORDER, part.a[1], a1_step, a2_step),
        ):
            if width:
                h, k = order[i]
                if h == 1:
                    first(k)
                second(h, k)

    def last():
        for book, h, slots in ((a2, 4, a_slots), (b2, 2, b_slots)):
            if book:
                for k in range(len(slots)):
                    for _, d in SIDES:
                        book[h, k, d].wait_recv()

    return [functools.partial(step, i) for i in range(16)] + [last]


def scatter_steps(place, start, part_sums, result, land_a, land_b, part):
    a1, b1, a2, b2 = {}, {}, {}, {}
    a_slots = (2, 1, -1, 0)
    b_slots = (4, 3, -3, 2, -2, 1, -1, 0)
    b_order = [(1, k) for k in range(4)]
    b_order += [(2, 0), (1, 4), (2, 1), (1, 5), (2, 2), (1, 6), (2, 3), (1, 7)] + [(2, k) for k in range(4, 8)]
    at = place.slot
    used = {"a": {}, "b": {}}

    def send(book, key, slot, piece, to, kind):
        land = land_a if kind == "a" else land_b
        offset = piece[0] - (part.a if kind == "a" else part.b)[0]
        index = used[kind].setdefault(key, len(used[kind]))

        def there():
            return land.at[index, :, pl.ds(offset, piece[1])]

        book[key] = (start(lambda: cols(part_sums, slot, piece), there, to), there, piece)

    def add(book, key, slot):
        copy, there, piece = book[key]
        copy.wait_recv()
        own = cols(part_sums, slot, piece)
        own[...] += there()[...]

    def a1_step(h, k, sides=SIDES):
        for side, d in sides:
            slot = at(a_slots[k], d * (5 - h))
            if h > 1:
                add(a1, (h - 1, k, d), slot)
            piece = part.a_half[side] if h == 1 else part.a
            send(a1, (h, k, d), slot, piece, place.along_z(d), "a")

    def b1_step(h, k, sides=SIDES):
        for side, d in sides:
            slot = at(d * (3 - h), b_slots[k])
            if h == 2:
                add(b1, (1, k, d), slot)
            piece = part.b_half[side] if h == 1 else part.b
            send(b1, (h, k, d), slot, piece, place.along_y(d), "b")

    def a1_end(k):
        for _, d in SIDES:
            add(a1, (4, k, d), at(a_slots[k], 0))

    def b1_end(k):
        for _, d in SIDES:
            add(b1, (2, k, d), at(0, b_slots[k]))

    def a2_step(k):
        d = a_slots[k]
        send(a2, d, at(d, 0), part.a, place.along_y(d), "a")

    def b2_step(k):
        d = b_slots[k]
        if d == 4:
            for side, way in SIDES:
                send(b2, 4 * way, at(0, 4), part.b_half[side], place.along_z(2 * way), "b")
            return
        if abs(d) == 2:
            add(b2, 2 * d, at(0, d))
            add(b2, 3 * d // 2, at(0, d))
        send(b2, d, at(0, d), part.b, place.along_z(d // 3 if abs(d) == 3 else d), "b")

    def end(book, keys, piece):
        own = at(0, 0)
        for key in keys:
            add(book, key, own)
        cols(result, own, piece)[...] = cols(part_sums, own, piece)[...]

    early = SIDES[:1]

    def before():
        for k in range(4):
            if part.a[1]:
                a1_step(1, k, early)
            else:
                b1_step(1, k, early)

    def step(i):
        if i < 16:
            late = SIDES[1:] if i < 4 else SIDES
            if part.b[1]:
                b1_step(*b_order[i], SIDES if part.a[1] else late)
            if part.a[1]:
                a1_step(*A_ORDER[i], late)
        for k in range(8):
            if part.b[1] and i == b_order.index((2, k)) + 2:
                b1_end(k)
                if k < 7:
                    b2_step(k)
        for k in range(4):
            if part.a[1] and i == A_ORDER.index((4, k)) + 2:
                a1_end(k)
                if k < 3:
                    a2_step(k)
        if i == 19:
            if part.b[1]:
                end(b2, (2, -2, 1, -1), part.b)
            if part.a[1]:
                end(a2, (2, 1, -1), part.a)

    return [before], [functools.partial(step, i) for i in range(20)]


GATHER_WIRES = 3 + 8 + 32 + 32
SCATTER_WIRES = 32 + 32 + 3 + 8
OTHER_WIRES = 11 + 24 + 4
WIRES = GATHER_WIRES + SCATTER_WIRES + OTHER_WIRES


def column_block(c):
    return pl.ds(pl.multiple_of(c * BLOCK, BLOCK), BLOCK)


def block_pieces(body, begin, end, size):
    def piece(first, last):
        def run():
            @pl.loop(first, last, unroll=last - first)
            def _(c):
                body(column_block(c))

        return run

    return [piece(c, min(c + size, end)) for c in range(begin, end, size)]


def in_order(timed):
    for _, _, step in sorted((key, n, step) for n, (key, step) in enumerate(timed)):
        step()


def at_times(steps, begin, apart=1.0):
    return [(begin + apart * i, step) for i, step in enumerate(steps)]


def core(
    momentum, gradient, basis,
    coeffs, ortho, inverse, new_basis,
    q_all, w_part, w_all, land_a, land_b, m_buf, g_buf, b_high, b_low, c_buf,
    p_part, p_core, p_x, p_all, p_t, gram_own, gram_z, gram_y, work, linv, linv_high, linv_low, norm_sum, norm_core, norm_x,
    send, recv, local,
):
    place = Place()
    wires = Wires(send, recv, POOL, OTHER_POOL)
    core_wires = [Wires(send, recv, 0, POOL) for _ in PARTS]
    other_start = wires.range(GATHER_WIRES + SCATTER_WIRES, OTHER_WIRES)

    def start(src, dst, to):
        return other_start(lambda: src, lambda: dst, to)

    def by_core(lists):
        def both(steps):
            def run():
                for index, step in enumerate(steps):
                    pl.when(core_index == index)(step)

            return run

        return [both(steps) for steps in zip(*lists, strict=True)]

    def gather(buf):
        return by_core(
            [gather_steps(place, w.range(0, GATHER_WIRES), buf, part) for w, part in zip(core_wires, PARTS)]
        )
    f, t, y, z, x, core_index = place.f, place.t, place.y, place.z, place.x, place.c

    loads = [
        pltpu.make_async_copy(basis, q_all.at[f], local.at[0]),
        pltpu.make_async_copy(momentum, m_buf, local.at[1]),
        pltpu.make_async_copy(gradient, g_buf, local.at[2]),
    ]
    for load in loads:
        load.start()

    barrier = pltpu.get_barrier_semaphore()
    peers = (
        [place.along_y(d) for d in range(1, Y)]
        + [place.along_z(d) for d in range(1, Z)]
        + [place.along_x(d) for d in range(1, 4)]
        + [place.other_core()]
    )
    for peer in peers:
        pl.semaphore_signal(barrier, inc=1, device_id=peer, device_id_type=MESH)
    pl.semaphore_wait(barrier, len(peers))

    def split_block(at):
        high, low = split(m_buf[:, at] + g_buf[:, at].astype(f32))
        b_high[:, at] = high
        b_low[:, at] = low

    def project(at):
        q = split(q_all[:, :, at].reshape(RANK, BLOCK))
        p_part[...] += dot3((b_high[:, at], b_low[:, at]), q, ((1,), (1,))).reshape(T, M // T, RANK)

    def loaded():
        p_part[...] = jnp.zeros_like(p_part)
        loads[1].wait()
        loads[2].wait()

    blocks = N // BLOCK
    loads[0].wait()
    timed = at_times(gather(q_all), 0)
    timed += [(1.4, loaded)]
    timed += at_times(block_pieces(split_block, 0, blocks, 1), 1.5)
    in_order(timed)
    for piece in block_pieces(project, 0, blocks, blocks):
        piece()

    mine = 4 * core_index
    copy = start(p_part.at[pl.ds(4 - mine, 4)], p_core, place.other_core())
    copy.wait_recv()
    p_core[...] += p_part[pl.ds(mine, 4)]
    copies = [
        start(p_core.at[(x + d) % 4], p_x.at[x], place.along_x(d)) for d in (2, 1, 3)
    ]
    p_x[x] = p_core[x]
    for copy in copies:
        copy.wait_recv()
    p_all[mine + x] = (p_x[0] + p_x[1]) + (p_x[2] + p_x[3])

    def copy_p(block, to):
        return start(p_all.at[block], p_all.at[block], to)

    copies = [copy_p(mine + x, place.along_x(d)) for d in (2, 1, 3)]
    core_copies = [copy_p(mine + x, place.other_core())]
    for d, copy in ((1, copies[1]), (3, copies[2]), (2, copies[0])):
        copy.wait_recv()
        core_copies.append(copy_p(mine + (x - d + 4) % 4, place.other_core()))
    for copy in core_copies:
        copy.wait_recv()

    proj = p_all[...].reshape(M, RANK)
    p_t[...] = proj.T
    rows = p_t[pl.ds(pl.multiple_of(t * (RANK // T), RANK // T), RANK // T), :]
    own = exact(rows, proj)
    for j in range(Z):
        gram_own[j] = own[8 * (j // 2) : 8 * (j // 2) + 8, 128 * (j % 2) : 128 * (j % 2) + 128]
    gram_copies = [
        start(gram_own.at[(z + d) % Z], gram_z.at[z], place.along_z(d)) for d in range(1, Z)
    ]
    gram_sent = list(gram_copies)
    gram_z[z] = gram_own[z]

    pt_split = split(p_t[...])

    def coefficients(at):
        w_part[:, :, at] = dot3(pt_split, (b_high[:, at], b_low[:, at])).reshape(F, R, BLOCK)

    scatters = [
        scatter_steps(place, w.range(GATHER_WIRES, SCATTER_WIRES), w_part, w_all, land_a, land_b, part)
        for w, part in zip(core_wires, PARTS)
    ]
    before, after = (by_core(lists) for lists in zip(*scatters))
    (early,) = block_pieces(coefficients, 0, EARLY, EARLY)
    (late,) = block_pieces(coefficients, EARLY, blocks, blocks)
    early()
    before[0]()
    late()

    def summed(ref, count):
        total = ref[0]
        for i in range(1, count):
            total = total + ref[i]
        return total

    def arrived(*sent):
        for copy in gram_copies:
            copy.wait_recv()
        gram_copies.clear()

    def send_gram(copies):
        gram_copies.extend(copies)
        gram_sent.extend(copies)

    tile = (4 * t + z // 2, slice(None), pl.ds(pl.multiple_of(z % 2 * 128, 128), 128))

    def gram_rows(owner):
        return work.at[pl.ds(4 * owner, 4), :, pl.ds(0, RANK)]

    def to_other_core(owner):
        return start(gram_rows(owner), gram_rows(owner), place.other_core())

    def gram_1():
        arrived()
        gram_y[y] = summed(gram_z, Z)
        send_gram([start(gram_y.at[y], gram_y.at[y], place.along_y(d)) for d in range(1, Y)])

    def gram_2():
        arrived()
        work[tile] = summed(gram_y, Y)
        send_gram([start(work.at[tile], work.at[tile], place.along_z(d)) for d in range(1, Z)])

    def gram_3():
        arrived()
        send_gram([start(gram_rows(t), gram_rows(t), place.along_x(d)) for d in range(1, 4)])

    def gram_4():
        arrived()
        send_gram([to_other_core((x + d) % 4 * 2 + core_index) for d in range(4)])

    def gram_5():
        arrived()
        for copy in gram_sent:
            copy.wait_send()
        row = lax.broadcasted_iota(jnp.int32, (RANK, RANK), 0)
        lane = lax.broadcasted_iota(jnp.int32, (RANK, RANK), 1)
        work[:, :, RANK:] = jnp.where(row == lane, 1.0, 0.0).astype(f32).reshape(F, R, RANK)

    lane = lax.broadcasted_iota(jnp.int32, (NB, 128), 1)
    sub = lax.broadcasted_iota(jnp.int32, (NB, 128), 0)

    def panel(p):
        tiles = NB // R
        here = work[pl.ds(p * tiles, tiles)].reshape(NB, 2 * RANK)
        start = p * NB
        low_half = jnp.where(start < 128, here[:, :128], here[:, 128:256])
        block = pltpu.roll(low_half, (128 - start % 128) % 128, 1)
        columns = [jnp.broadcast_to(block[:, j : j + 1], (NB, 128)) for j in range(NB)]
        right = jnp.where(lane == sub, 1.0, 0.0).astype(f32)
        diag = jnp.ones((NB, 128), f32)
        for j in range(NB):
            pivot = jnp.broadcast_to(columns[j][j : j + 1, :], (NB, 128))
            diag = jnp.where(sub == j, pivot, diag)
            if j < NB - 1:
                factor = jnp.where(sub > j, columns[j] * (1.0 / pivot), 0.0)
                for i in range(j + 1, NB):
                    columns[i] = columns[i] - factor * columns[i][j : j + 1, :]
                right = right - factor * right[j : j + 1, :]
        right = right * lax.rsqrt(diag)
        done = right[:, 0:1] * here[0:1, :]
        for j in range(1, NB):
            done = done + right[:, j : j + 1] * here[j : j + 1, :]
        linv[pl.ds(p * tiles, tiles)] = done[:, RANK:].reshape(tiles, R, RANK)
        high = done.astype(bf16).astype(f32)
        mid = (done - high).astype(bf16).astype(f32)
        low = (done - high) - mid
        left = jnp.concatenate([v[:, :RANK] for v in (high, high, mid, high, low, mid)]).astype(bf16)
        beside = jnp.concatenate([high, mid, high, low, high, mid]).astype(bf16)
        work[...] -= dot(left, beside, ((0,), (0,))).reshape(F, R, 2 * RANK)

    def panels(begin, end):
        def run():
            @pl.loop(begin, end)
            def _(p):
                panel(p)

        return run

    def prepare():
        linv_high[...], linv_low[...] = split(linv[...].reshape(RANK, RANK))
        norm_sum[...] = jnp.zeros_like(norm_sum)

    def multiply(at):
        part = dot3((linv_high[...], linv_low[...]), split(w_all[:, :, at].reshape(RANK, BLOCK)))
        c_buf[:, at] = part
        squares = part * part
        norm_sum[...] += squares[:, :128] + squares[:, 128:]

    timed = at_times(after + gather(w_all), 0)
    timed += [(5.5, gram_1), (8.5, gram_2), (12.5, gram_3), (15.5, gram_4), (17.5, gram_5)]
    timed += at_times([panels(p, p + 1) for p in range(RANK // NB)], 18.5)
    timed += [(35.5, prepare)]
    in_order(timed)

    stores = []
    for size, piece in zip((7, 6), block_pieces(multiply, 0, blocks, 7), strict=True):
        piece()
        at = pl.ds(len(stores) * 7 * BLOCK, size * BLOCK)
        stores.append(pltpu.make_async_copy(c_buf.at[:, at], coeffs.at[:, at], local.at[len(stores)]))
        stores[-1].start()
    own_norms = jnp.sum(norm_sum[...].T, axis=0, keepdims=True)
    norm_core[0, 0:8] = jnp.broadcast_to(own_norms[:, :128], (8, 128))
    norm_core[0, 8:16] = jnp.broadcast_to(own_norms[:, 128:], (8, 128))
    copy = start(norm_core.at[0], norm_core.at[1], place.other_core())
    copy.wait_recv()
    norm_x[x] = norm_core[0] + norm_core[1]
    copies = [start(norm_x.at[x], norm_x.at[x], place.along_x(d)) for d in (2, 1, 3)]
    ortho[...] = exact(p_all[...].reshape(M, RANK), linv[...].reshape(RANK, RANK), ((1,), (1,)))
    for copy in copies:
        copy.wait_recv()
    scale = lax.rsqrt((norm_x[0] + norm_x[1]) + (norm_x[2] + norm_x[3]) + norm_eps)
    inverse_row = jnp.concatenate([scale[0:8], scale[8:16]], axis=1)
    inverse[...] = inverse_row
    lanes = lax.broadcasted_iota(jnp.int32, (R, RANK), 1)
    subs = lax.broadcasted_iota(jnp.int32, (R, RANK), 0)
    own_inverse = jnp.sum(jnp.where(lanes == subs + f * R, inverse_row, 0.0), axis=1, keepdims=True)
    new_basis[...] = c_buf[pl.ds(pl.multiple_of(f * R, R), R), :] * own_inverse
    for copy in stores:
        copy.wait()
    wires.drain()
    by_core([[w.drain] for w in core_wires])[0]()


def core_call(momentum, gradient, basis):
    any_space = pl.BlockSpec(memory_space=pl.ANY)
    vmem = pl.BlockSpec(memory_space=pltpu.VMEM)
    return pl.pallas_call(
        core,
        out_shape=(
            jax.ShapeDtypeStruct((RANK, N), f32),
            jax.ShapeDtypeStruct((M, RANK), f32),
            jax.ShapeDtypeStruct((8, RANK), f32),
            jax.ShapeDtypeStruct((R, N), f32),
        ),
        in_specs=[any_space] * 3,
        out_specs=(any_space, vmem, vmem, vmem),
        scratch_shapes=[
            pltpu.VMEM((F, R, N), f32),
            pltpu.VMEM((F, R, N), f32),
            pltpu.VMEM((F, R, N), f32),
            pltpu.VMEM((A_LANDS, R, max(part.a[1] for part in PARTS)), f32),
            pltpu.VMEM((B_LANDS, R, max(part.b[1] for part in PARTS)), f32),
            pltpu.VMEM((M, N), f32),
            pltpu.VMEM((M, N), bf16),
            pltpu.VMEM((M, N), bf16),
            pltpu.VMEM((M, N), bf16),
            pltpu.VMEM((RANK, N), f32),
            pltpu.VMEM((T, M // T, RANK), f32),
            pltpu.VMEM((T // 2, M // T, RANK), f32),
            pltpu.VMEM((T // 2, M // T, RANK), f32),
            pltpu.VMEM((T, M // T, RANK), f32),
            pltpu.VMEM((RANK, M), f32),
            pltpu.VMEM((Z, 8, 128), f32),
            pltpu.VMEM((Z, 8, 128), f32),
            pltpu.VMEM((Y, 8, 128), f32),
            pltpu.VMEM((F, R, 2 * RANK), f32),
            pltpu.VMEM((F, R, RANK), f32),
            pltpu.VMEM((RANK, RANK), bf16),
            pltpu.VMEM((RANK, RANK), bf16),
            pltpu.VMEM((RANK, 128), f32),
            pltpu.VMEM((2, 16, 128), f32),
            pltpu.VMEM((4, 16, 128), f32),
            pltpu.SemaphoreType.DMA((POOL + OTHER_POOL,)),
            pltpu.SemaphoreType.DMA((WIRES,)),
            pltpu.SemaphoreType.DMA((3,)),
        ],
        compiler_params=pltpu.CompilerParams(
            collective_id=0, has_side_effects=True, vmem_limit_bytes=60 * 2**20
        ),
        name="core",
    )(momentum, gradient, basis)


def update(momentum, gradient, coeffs, ortho, inverse, own_basis, new_momentum, step, new_basis):
    new_basis[...] = own_basis[...]
    buffer = momentum[...] + gradient[...].astype(f32)
    high, low = split(coeffs[...])
    basis = ortho[...]
    new_momentum[...] = buffer - (1.0 - momentum_decay) * dot(basis.astype(bf16), high)
    scale = (ROWS * COLS / RANK) ** 0.5
    scaled = split(basis * (inverse[0:1, :] * scale))
    step[...] = dot3(scaled, (high, low)).astype(bf16)


def update_call(momentum, gradient, coeffs, ortho, inverse, own_basis):
    wide = N // 2

    def block(rows):
        return pl.BlockSpec((rows, wide), lambda c: (0, c))

    return pl.pallas_call(
        update,
        grid=(N // wide,),
        out_shape=(
            jax.ShapeDtypeStruct((M, N), f32),
            jax.ShapeDtypeStruct((M, N), bf16),
            jax.ShapeDtypeStruct((R, N), f32),
        ),
        in_specs=[
            block(M), block(M), block(RANK),
            pl.BlockSpec((M, RANK), lambda c: (0, 0)),
            pl.BlockSpec((8, RANK), lambda c: (0, 0)),
            block(R),
        ],
        out_specs=(block(M), block(M), block(R)),
        compiler_params=pltpu.CompilerParams(vmem_limit_bytes=60 * 2**20),
        name="update",
    )(momentum, gradient, coeffs, ortho, inverse, own_basis)


def on_device(momentum, gradient, basis):
    coeffs, ortho, inverse, own_basis = core_call(momentum, gradient, basis)
    new_momentum, step, new_basis = update_call(momentum, gradient, coeffs, ortho, inverse, own_basis)
    return (new_momentum, new_basis, step)


def solution(mesh):
    placed = (P("fsdp", "tp"), P("fsdp", "tp"), P("fsdp", "tp"))
    return jax.shard_map(
        on_device,
        mesh=mesh,
        in_specs=placed,
        out_specs=(P("fsdp", "tp"), P("fsdp", "tp"), P("fsdp", "tp")),
        check_vma=False,
    )
```

```python
import functools

import jax
import jax.numpy as jnp
from jax import lax
from jax.experimental import pallas as pl
from jax.experimental.pallas import tpu as pltpu
from jax.sharding import PartitionSpec as P

ROWS = 8192
COLS = 26624
RANK = 256

momentum_decay = 0.95
norm_eps = 1e-06

Y, Z, T = 4, 8, 8
F = Y * Z
M = ROWS // F
N = COLS // T
R = RANK // F
BLOCK = 256
NB = 16


class Part:
    def __init__(self, begin, size, cut):
        self.begin, self.size = begin, size
        self.a, self.b = (begin, cut), (begin + cut, size - cut)
        self.a_half, self.b_half = self.halves(self.a), self.halves(self.b)

    @staticmethod
    def halves(part):
        first = (part[1] // 128 + 1) // 2 * 128
        return (part[0], first), (part[0] + first, part[1] - first)


PARTS = (Part(0, N, 2560), Part(0, N, 0))
A_LANDS = 4 * 4 * 2 + 2 * 2
B_LANDS = 2 * 8 * 2 + 4 * 2
POOL = 32
OTHER_POOL = 16
EARLY = 7

MESH = pl.DeviceIdType.MESH
f32, bf16 = jnp.float32, jnp.bfloat16


def split(value):
    high = value.astype(bf16)
    return high, (value - high.astype(f32)).astype(bf16)


def dot(left, right, dims=((1,), (0,))):
    return lax.dot_general(left, right, (dims, ((), ())), preferred_element_type=f32)


def dot3(left, right, dims=((1,), (0,))):
    (lh, ll), (rh, rl) = left, right
    return dot(lh, rh, dims) + (dot(lh, rl, dims) + dot(ll, rh, dims))


def exact(left, right, dims=((1,), (0,))):
    return lax.dot_general(
        left, right, (dims, ((), ())), precision=lax.Precision.HIGHEST, preferred_element_type=f32
    )


class Copy:
    def __init__(self, make):
        self.make, self.sent = make, False

    def start(self):
        self.make().start()

    def wait_recv(self):
        self.make().wait_recv()

    def wait_send(self):
        if not self.sent:
            self.make().wait_send()
        self.sent = True


class Wires:
    def __init__(self, send, recv, first, size):
        self.send, self.recv, self.first, self.size = send, recv, first, size
        self.last, self.used = {}, 0

    def range(self, begin, count):
        indices = iter(range(begin, begin + count))
        return lambda src, dst, to: self.start(src, dst, to, next(indices))

    def start(self, src, dst, to, index):
        place = self.first + self.used % self.size
        self.used += 1
        if place in self.last:
            self.last[place].wait_send()
        copy = Copy(
            lambda: pltpu.make_async_remote_copy(
                src_ref=src(),
                dst_ref=dst(),
                send_sem=self.send.at[place],
                recv_sem=self.recv.at[index],
                device_id=to,
                device_id_type=MESH,
            )
        )
        copy.start()
        self.last[place] = copy
        return copy

    def drain(self):
        for copy in self.last.values():
            copy.wait_send()


class Place:
    def __init__(self):
        self.f = lax.axis_index("fsdp")
        self.t = lax.axis_index("tp")
        self.y, self.z = self.f // Z, self.f % Z
        self.x, self.c = self.t // 2, self.t % 2
        self.slots = {
            (dy, dz): (self.y + dy) % Y * Z + (self.z + dz) % Z for dy in range(Y) for dz in range(Z)
        }

    def slot(self, dy, dz):
        return self.slots[dy % Y, dz % Z]

    def along_y(self, d):
        return {"fsdp": self.slot(d, 0)}

    def along_z(self, d):
        return {"fsdp": self.slot(0, d)}

    def along_x(self, d):
        return {"tp": (self.x + d) % 4 * 2 + self.c}

    def other_core(self):
        return {"tp": self.x * 2 + 1 - self.c}


def cols(ref, slot, part):
    return ref.at[slot, :, pl.ds(part[0], part[1])]


SIDES = ((0, 1), (1, -1))
A_ORDER = [(h, k) for h in range(1, 5) for k in range(4)]


def gather_steps(place, start, buf, part):
    a1, b1, a2, b2 = {}, {}, {}, {}
    a_slots = (0, -1, 1, 2)
    b_slots = (0, -1, 1, -2, 2, -3, 3, 4)
    b_order = [(1, k) for k in range(5)]
    b_order += [(2, 0), (1, 5), (2, 1), (1, 6), (2, 2), (1, 7)] + [(2, k) for k in range(3, 8)]
    at = place.slot

    def send(book, key, slot, piece, to):
        def here():
            return cols(buf, slot, piece)

        book[key] = start(here, here, to)

    def a1_step(k):
        if k == 0:
            for d in (2, 1, -1):
                send(a1, d, at(0, 0), part.a, place.along_y(d))
        else:
            a1[-a_slots[k] if k < 3 else 2].wait_recv()

    def a2_step(h, k):
        for side, d in SIDES:
            if h > 1:
                a2[h - 1, k, d].wait_recv()
            piece = part.a_half[side] if h == 4 else part.a
            send(a2, (h, k, d), at(a_slots[k], -d * (h - 1)), piece, place.along_z(d))

    def b1_step(k):
        if k == 0:
            for d in (2, -2, 1, -1):
                send(b1, d, at(0, 0), part.b, place.along_z(d))
        elif k < 7:
            b1[-b_slots[k]].wait_recv()
            if k in (3, 4):
                side, d = SIDES[k - 3]
                send(b1, 4 * d, at(0, -2 * d), part.b_half[side], place.along_z(2 * d))
                send(b1, 3 * d, at(0, -2 * d), part.b, place.along_z(d))
        else:
            b1[4].wait_recv()
            b1[-4].wait_recv()

    def b2_step(h, k):
        for side, d in SIDES:
            if h == 2:
                b2[1, k, d].wait_recv()
            piece = part.b_half[side] if h == 2 else part.b
            send(b2, (h, k, d), at(-d * (h - 1), b_slots[k]), piece, place.along_y(d))

    def step(i):
        for order, width, first, second in (
            (b_order, part.b[1], b1_step, b2_step),
            (A_ORDER, part.a[1], a1_step, a2_step),
        ):
            if width:
                h, k = order[i]
                if h == 1:
                    first(k)
                second(h, k)

    def last():
        for book, h, slots in ((a2, 4, a_slots), (b2, 2, b_slots)):
            if book:
                for k in range(len(slots)):
                    for _, d in SIDES:
                        book[h, k, d].wait_recv()

    return [functools.partial(step, i) for i in range(16)] + [last]


def scatter_steps(place, start, part_sums, result, land_a, land_b, part):
    a1, b1, a2, b2 = {}, {}, {}, {}
    a_slots = (2, 1, -1, 0)
    b_slots = (4, 3, -3, 2, -2, 1, -1, 0)
    b_order = [(1, k) for k in range(4)]
    b_order += [(2, 0), (1, 4), (2, 1), (1, 5), (2, 2), (1, 6), (2, 3), (1, 7)] + [(2, k) for k in range(4, 8)]
    at = place.slot
    used = {"a": {}, "b": {}}

    def send(book, key, slot, piece, to, kind):
        land = land_a if kind == "a" else land_b
        offset = piece[0] - (part.a if kind == "a" else part.b)[0]
        index = used[kind].setdefault(key, len(used[kind]))

        def there():
            return land.at[index, :, pl.ds(offset, piece[1])]

        book[key] = (start(lambda: cols(part_sums, slot, piece), there, to), there, piece)

    def add(book, key, slot):
        copy, there, piece = book[key]
        copy.wait_recv()
        own = cols(part_sums, slot, piece)
        own[...] += there()[...]

    def a1_step(h, k, sides=SIDES):
        for side, d in sides:
            slot = at(a_slots[k], d * (5 - h))
            if h > 1:
                add(a1, (h - 1, k, d), slot)
            piece = part.a_half[side] if h == 1 else part.a
            send(a1, (h, k, d), slot, piece, place.along_z(d), "a")

    def b1_step(h, k, sides=SIDES):
        for side, d in sides:
            slot = at(d * (3 - h), b_slots[k])
            if h == 2:
                add(b1, (1, k, d), slot)
            piece = part.b_half[side] if h == 1 else part.b
            send(b1, (h, k, d), slot, piece, place.along_y(d), "b")

    def a1_end(k):
        for _, d in SIDES:
            add(a1, (4, k, d), at(a_slots[k], 0))

    def b1_end(k):
        for _, d in SIDES:
            add(b1, (2, k, d), at(0, b_slots[k]))

    def a2_step(k):
        d = a_slots[k]
        send(a2, d, at(d, 0), part.a, place.along_y(d), "a")

    def b2_step(k):
        d = b_slots[k]
        if d == 4:
            for side, way in SIDES:
                send(b2, 4 * way, at(0, 4), part.b_half[side], place.along_z(2 * way), "b")
            return
        if abs(d) == 2:
            add(b2, 2 * d, at(0, d))
            add(b2, 3 * d // 2, at(0, d))
        send(b2, d, at(0, d), part.b, place.along_z(d // 3 if abs(d) == 3 else d), "b")

    def end(book, keys, piece):
        own = at(0, 0)
        for key in keys:
            add(book, key, own)
        cols(result, own, piece)[...] = cols(part_sums, own, piece)[...]

    early = SIDES[:1]

    def before():
        for k in range(4):
            if part.a[1]:
                a1_step(1, k, early)
            else:
                b1_step(1, k, early)

    def step(i):
        if i < 16:
            late = SIDES[1:] if i < 4 else SIDES
            if part.b[1]:
                b1_step(*b_order[i], SIDES if part.a[1] else late)
            if part.a[1]:
                a1_step(*A_ORDER[i], late)
        for k in range(8):
            if part.b[1] and i == b_order.index((2, k)) + 2:
                b1_end(k)
                if k < 7:
                    b2_step(k)
        for k in range(4):
            if part.a[1] and i == A_ORDER.index((4, k)) + 2:
                a1_end(k)
                if k < 3:
                    a2_step(k)
        if i == 19:
            if part.b[1]:
                end(b2, (2, -2, 1, -1), part.b)
            if part.a[1]:
                end(a2, (2, 1, -1), part.a)

    return [before], [functools.partial(step, i) for i in range(20)]


GATHER_WIRES = 3 + 8 + 32 + 32
SCATTER_WIRES = 32 + 32 + 3 + 8
OTHER_WIRES = 11 + 24 + 4
WIRES = GATHER_WIRES + SCATTER_WIRES + OTHER_WIRES


def column_block(c):
    return pl.ds(pl.multiple_of(c * BLOCK, BLOCK), BLOCK)


def block_pieces(body, begin, end, size):
    def piece(first, last):
        def run():
            @pl.loop(first, last, unroll=last - first)
            def _(c):
                body(column_block(c))

        return run

    return [piece(c, min(c + size, end)) for c in range(begin, end, size)]


def in_order(timed):
    for _, _, step in sorted((key, n, step) for n, (key, step) in enumerate(timed)):
        step()


def at_times(steps, begin, apart=1.0):
    return [(begin + apart * i, step) for i, step in enumerate(steps)]


def core(
    momentum, gradient, basis,
    coeffs, ortho, inverse, new_basis,
    q_all, w_part, w_all, land_a, land_b, m_buf, g_buf, b_high, b_low, c_buf,
    p_part, p_core, p_x, p_all, p_t, gram_own, gram_z, gram_y, work, linv, linv_high, linv_low, norm_sum, norm_core, norm_x,
    send, recv, local,
):
    place = Place()
    wires = Wires(send, recv, POOL, OTHER_POOL)
    core_wires = [Wires(send, recv, 0, POOL) for _ in PARTS]
    other_start = wires.range(GATHER_WIRES + SCATTER_WIRES, OTHER_WIRES)

    def start(src, dst, to):
        return other_start(lambda: src, lambda: dst, to)

    def by_core(lists):
        def both(steps):
            def run():
                for index, step in enumerate(steps):
                    pl.when(core_index == index)(step)

            return run

        return [both(steps) for steps in zip(*lists, strict=True)]

    def gather(buf):
        return by_core(
            [gather_steps(place, w.range(0, GATHER_WIRES), buf, part) for w, part in zip(core_wires, PARTS)]
        )
    f, t, y, z, x, core_index = place.f, place.t, place.y, place.z, place.x, place.c

    loads = [
        pltpu.make_async_copy(basis, q_all.at[f], local.at[0]),
        pltpu.make_async_copy(momentum, m_buf, local.at[1]),
        pltpu.make_async_copy(gradient, g_buf, local.at[2]),
    ]
    for load in loads:
        load.start()

    barrier = pltpu.get_barrier_semaphore()
    peers = (
        [place.along_y(d) for d in range(1, Y)]
        + [place.along_z(d) for d in range(1, Z)]
        + [place.along_x(d) for d in range(1, 4)]
        + [place.other_core()]
    )
    for peer in peers:
        pl.semaphore_signal(barrier, inc=1, device_id=peer, device_id_type=MESH)
    pl.semaphore_wait(barrier, len(peers))

    def split_block(at):
        high, low = split(m_buf[:, at] + g_buf[:, at].astype(f32))
        b_high[:, at] = high
        b_low[:, at] = low

    def project(at):
        q = split(q_all[:, :, at].reshape(RANK, BLOCK))
        p_part[...] += dot3((b_high[:, at], b_low[:, at]), q, ((1,), (1,))).reshape(T, M // T, RANK)

    def loaded():
        p_part[...] = jnp.zeros_like(p_part)
        loads[1].wait()
        loads[2].wait()

    blocks = N // BLOCK
    loads[0].wait()
    timed = at_times(gather(q_all), 0)
    timed += [(1.4, loaded)]
    timed += at_times(block_pieces(split_block, 0, blocks, 1), 1.5)
    in_order(timed)
    for piece in block_pieces(project, 0, blocks, blocks):
        piece()

    mine = 4 * core_index
    copy = start(p_part.at[pl.ds(4 - mine, 4)], p_core, place.other_core())
    copy.wait_recv()
    p_core[...] += p_part[pl.ds(mine, 4)]
    copies = [
        start(p_core.at[(x + d) % 4], p_x.at[x], place.along_x(d)) for d in (2, 1, 3)
    ]
    p_x[x] = p_core[x]
    for copy in copies:
        copy.wait_recv()
    p_all[mine + x] = (p_x[0] + p_x[1]) + (p_x[2] + p_x[3])

    def copy_p(block, to):
        return start(p_all.at[block], p_all.at[block], to)

    copies = [copy_p(mine + x, place.along_x(d)) for d in (2, 1, 3)]
    core_copies = [copy_p(mine + x, place.other_core())]
    for d, copy in ((1, copies[1]), (3, copies[2]), (2, copies[0])):
        copy.wait_recv()
        core_copies.append(copy_p(mine + (x - d + 4) % 4, place.other_core()))
    for copy in core_copies:
        copy.wait_recv()

    proj = p_all[...].reshape(M, RANK)
    p_t[...] = proj.T
    pt_split = split(p_t[...])

    def coefficients(at):
        w_part[:, :, at] = dot3(pt_split, (b_high[:, at], b_low[:, at])).reshape(F, R, BLOCK)

    scatters = [
        scatter_steps(place, w.range(GATHER_WIRES, SCATTER_WIRES), w_part, w_all, land_a, land_b, part)
        for w, part in zip(core_wires, PARTS)
    ]
    before, after = (by_core(lists) for lists in zip(*scatters))
    (early,) = block_pieces(coefficients, 0, EARLY, EARLY)
    (late,) = block_pieces(coefficients, EARLY, blocks, blocks)
    early()
    before[0]()
    rows = p_t[pl.ds(pl.multiple_of(t * (RANK // T), RANK // T), RANK // T), :]
    own = exact(rows, proj)
    for j in range(Z):
        gram_own[j] = own[8 * (j // 2) : 8 * (j // 2) + 8, 128 * (j % 2) : 128 * (j % 2) + 128]
    gram_copies = [
        start(gram_own.at[(z + d) % Z], gram_z.at[z], place.along_z(d)) for d in range(1, Z)
    ]
    gram_sent = list(gram_copies)
    gram_z[z] = gram_own[z]
    late()

    def summed(ref, count):
        total = ref[0]
        for i in range(1, count):
            total = total + ref[i]
        return total

    def arrived(*sent):
        for copy in gram_copies:
            copy.wait_recv()
        gram_copies.clear()

    def send_gram(copies):
        gram_copies.extend(copies)
        gram_sent.extend(copies)

    tile = (4 * t + z // 2, slice(None), pl.ds(pl.multiple_of(z % 2 * 128, 128), 128))

    def gram_rows(owner):
        return work.at[pl.ds(4 * owner, 4), :, pl.ds(0, RANK)]

    def to_other_core(owner):
        return start(gram_rows(owner), gram_rows(owner), place.other_core())

    def gram_1():
        arrived()
        gram_y[y] = summed(gram_z, Z)
        send_gram([start(gram_y.at[y], gram_y.at[y], place.along_y(d)) for d in range(1, Y)])

    def gram_2():
        arrived()
        work[tile] = summed(gram_y, Y)
        send_gram([start(work.at[tile], work.at[tile], place.along_z(d)) for d in range(1, Z)])

    def gram_3():
        arrived()
        send_gram([start(gram_rows(t), gram_rows(t), place.along_x(d)) for d in range(1, 4)])

    def gram_4():
        arrived()
        send_gram([to_other_core((x + d) % 4 * 2 + core_index) for d in range(4)])

    def gram_5():
        arrived()
        for copy in gram_sent:
            copy.wait_send()
        row = lax.broadcasted_iota(jnp.int32, (RANK, RANK), 0)
        lane = lax.broadcasted_iota(jnp.int32, (RANK, RANK), 1)
        work[:, :, RANK:] = jnp.where(row == lane, 1.0, 0.0).astype(f32).reshape(F, R, RANK)

    lane = lax.broadcasted_iota(jnp.int32, (NB, 128), 1)
    sub = lax.broadcasted_iota(jnp.int32, (NB, 128), 0)

    def panel(p):
        tiles = NB // R
        here = work[pl.ds(p * tiles, tiles)].reshape(NB, 2 * RANK)
        start = p * NB
        low_half = jnp.where(start < 128, here[:, :128], here[:, 128:256])
        block = pltpu.roll(low_half, (128 - start % 128) % 128, 1)
        columns = [jnp.broadcast_to(block[:, j : j + 1], (NB, 128)) for j in range(NB)]
        right = jnp.where(lane == sub, 1.0, 0.0).astype(f32)
        diag = jnp.ones((NB, 128), f32)
        for j in range(NB):
            pivot = jnp.broadcast_to(columns[j][j : j + 1, :], (NB, 128))
            diag = jnp.where(sub == j, pivot, diag)
            if j < NB - 1:
                factor = jnp.where(sub > j, columns[j] * (1.0 / pivot), 0.0)
                for i in range(j + 1, NB):
                    columns[i] = columns[i] - factor * columns[i][j : j + 1, :]
                right = right - factor * right[j : j + 1, :]
        right = right * lax.rsqrt(diag)
        done = right[:, 0:1] * here[0:1, :]
        for j in range(1, NB):
            done = done + right[:, j : j + 1] * here[j : j + 1, :]
        linv[pl.ds(p * tiles, tiles)] = done[:, RANK:].reshape(tiles, R, RANK)
        high = done.astype(bf16).astype(f32)
        mid = (done - high).astype(bf16).astype(f32)
        low = (done - high) - mid
        left = jnp.concatenate([v[:, :RANK] for v in (high, high, mid, high, low, mid)]).astype(bf16)
        beside = jnp.concatenate([high, mid, high, low, high, mid]).astype(bf16)
        work[...] -= dot(left, beside, ((0,), (0,))).reshape(F, R, 2 * RANK)

    def panels(begin, end):
        def run():
            @pl.loop(begin, end)
            def _(p):
                panel(p)

        return run

    def prepare():
        linv_high[...], linv_low[...] = split(linv[...].reshape(RANK, RANK))
        norm_sum[...] = jnp.zeros_like(norm_sum)

    def multiply(at):
        part = dot3((linv_high[...], linv_low[...]), split(w_all[:, :, at].reshape(RANK, BLOCK)))
        c_buf[:, at] = part
        squares = part * part
        norm_sum[...] += squares[:, :128] + squares[:, 128:]

    timed = at_times(after + gather(w_all), 0)
    timed += [(7.5, gram_1), (10.5, gram_2), (14.5, gram_3), (17.5, gram_4), (19.5, gram_5)]
    timed += at_times([panels(p, p + 1) for p in range(RANK // NB)], 20.5, 0.95)
    timed += [(35.5, prepare)]
    in_order(timed)

    stores = []
    for size, piece in zip((7, 6), block_pieces(multiply, 0, blocks, 7), strict=True):
        piece()
        at = pl.ds(len(stores) * 7 * BLOCK, size * BLOCK)
        stores.append(pltpu.make_async_copy(c_buf.at[:, at], coeffs.at[:, at], local.at[len(stores)]))
        stores[-1].start()
    own_norms = jnp.sum(norm_sum[...].T, axis=0, keepdims=True)
    norm_core[0, 0:8] = jnp.broadcast_to(own_norms[:, :128], (8, 128))
    norm_core[0, 8:16] = jnp.broadcast_to(own_norms[:, 128:], (8, 128))
    copy = start(norm_core.at[0], norm_core.at[1], place.other_core())
    copy.wait_recv()
    norm_x[x] = norm_core[0] + norm_core[1]
    copies = [start(norm_x.at[x], norm_x.at[x], place.along_x(d)) for d in (2, 1, 3)]
    ortho[...] = exact(p_all[...].reshape(M, RANK), linv[...].reshape(RANK, RANK), ((1,), (1,)))
    for copy in copies:
        copy.wait_recv()
    scale = lax.rsqrt((norm_x[0] + norm_x[1]) + (norm_x[2] + norm_x[3]) + norm_eps)
    inverse_row = jnp.concatenate([scale[0:8], scale[8:16]], axis=1)
    inverse[...] = inverse_row
    lanes = lax.broadcasted_iota(jnp.int32, (R, RANK), 1)
    subs = lax.broadcasted_iota(jnp.int32, (R, RANK), 0)
    own_inverse = jnp.sum(jnp.where(lanes == subs + f * R, inverse_row, 0.0), axis=1, keepdims=True)
    new_basis[...] = c_buf[pl.ds(pl.multiple_of(f * R, R), R), :] * own_inverse
    for copy in stores:
        copy.wait()
    wires.drain()
    by_core([[w.drain] for w in core_wires])[0]()


def core_call(momentum, gradient, basis):
    any_space = pl.BlockSpec(memory_space=pl.ANY)
    vmem = pl.BlockSpec(memory_space=pltpu.VMEM)
    return pl.pallas_call(
        core,
        out_shape=(
            jax.ShapeDtypeStruct((RANK, N), f32),
            jax.ShapeDtypeStruct((M, RANK), f32),
            jax.ShapeDtypeStruct((8, RANK), f32),
            jax.ShapeDtypeStruct((R, N), f32),
        ),
        in_specs=[any_space] * 3,
        out_specs=(any_space, vmem, vmem, vmem),
        scratch_shapes=[
            pltpu.VMEM((F, R, N), f32),
            pltpu.VMEM((F, R, N), f32),
            pltpu.VMEM((F, R, N), f32),
            pltpu.VMEM((A_LANDS, R, max(part.a[1] for part in PARTS)), f32),
            pltpu.VMEM((B_LANDS, R, max(part.b[1] for part in PARTS)), f32),
            pltpu.VMEM((M, N), f32),
            pltpu.VMEM((M, N), bf16),
            pltpu.VMEM((M, N), bf16),
            pltpu.VMEM((M, N), bf16),
            pltpu.VMEM((RANK, N), f32),
            pltpu.VMEM((T, M // T, RANK), f32),
            pltpu.VMEM((T // 2, M // T, RANK), f32),
            pltpu.VMEM((T // 2, M // T, RANK), f32),
            pltpu.VMEM((T, M // T, RANK), f32),
            pltpu.VMEM((RANK, M), f32),
            pltpu.VMEM((Z, 8, 128), f32),
            pltpu.VMEM((Z, 8, 128), f32),
            pltpu.VMEM((Y, 8, 128), f32),
            pltpu.VMEM((F, R, 2 * RANK), f32),
            pltpu.VMEM((F, R, RANK), f32),
            pltpu.VMEM((RANK, RANK), bf16),
            pltpu.VMEM((RANK, RANK), bf16),
            pltpu.VMEM((RANK, 128), f32),
            pltpu.VMEM((2, 16, 128), f32),
            pltpu.VMEM((4, 16, 128), f32),
            pltpu.SemaphoreType.DMA((POOL + OTHER_POOL,)),
            pltpu.SemaphoreType.DMA((WIRES,)),
            pltpu.SemaphoreType.DMA((3,)),
        ],
        compiler_params=pltpu.CompilerParams(
            collective_id=0, has_side_effects=True, vmem_limit_bytes=60 * 2**20
        ),
        name="core",
    )(momentum, gradient, basis)


def update(momentum, gradient, coeffs, ortho, inverse, own_basis, new_momentum, step, new_basis):
    new_basis[...] = own_basis[...]
    buffer = momentum[...] + gradient[...].astype(f32)
    high, low = split(coeffs[...])
    basis = ortho[...]
    new_momentum[...] = buffer - (1.0 - momentum_decay) * dot(basis.astype(bf16), high)
    scale = (ROWS * COLS / RANK) ** 0.5
    scaled = split(basis * (inverse[0:1, :] * scale))
    step[...] = dot3(scaled, (high, low)).astype(bf16)


def update_call(momentum, gradient, coeffs, ortho, inverse, own_basis):
    wide = N // 2

    def block(rows):
        return pl.BlockSpec((rows, wide), lambda c: (0, c))

    return pl.pallas_call(
        update,
        grid=(N // wide,),
        out_shape=(
            jax.ShapeDtypeStruct((M, N), f32),
            jax.ShapeDtypeStruct((M, N), bf16),
            jax.ShapeDtypeStruct((R, N), f32),
        ),
        in_specs=[
            block(M), block(M), block(RANK),
            pl.BlockSpec((M, RANK), lambda c: (0, 0)),
            pl.BlockSpec((8, RANK), lambda c: (0, 0)),
            block(R),
        ],
        out_specs=(block(M), block(M), block(R)),
        compiler_params=pltpu.CompilerParams(vmem_limit_bytes=60 * 2**20),
        name="update",
    )(momentum, gradient, coeffs, ortho, inverse, own_basis)


def on_device(momentum, gradient, basis):
    coeffs, ortho, inverse, own_basis = core_call(momentum, gradient, basis)
    new_momentum, step, new_basis = update_call(momentum, gradient, coeffs, ortho, inverse, own_basis)
    return (new_momentum, new_basis, step)


def solution(mesh):
    placed = (P("fsdp", "tp"), P("fsdp", "tp"), P("fsdp", "tp"))
    return jax.shard_map(
        on_device,
        mesh=mesh,
        in_specs=placed,
        out_specs=(P("fsdp", "tp"), P("fsdp", "tp"), P("fsdp", "tp")),
        check_vma=False,
    )
```
